32 devices in a mesh: grp: 2 (over x), own: 16 (over z, y, core).
Axes of the slice: x: 2, y: 2, z: 4, core: 2. Of those that a mesh axis runs over, the one named last changes fastest.
Arguments:
- tokens: bfloat16 [4096, 8192], P(('grp', 'own')), parts along dimension 0, may hold values from -6 to 6
- adapter_index_rows: int32 [4096, 1], P(('grp', 'own')), parts along dimension 0, may hold values from 0 to 31; in each aligned block of 128 rows (0 to 127, 128 to 255, ...) at most 8 rows name the same one
- adapter_pool_position: int32 [64], P('grp'), parts along dimension 0, may hold values from 0 to 31, each once
- base_value_matrix: bfloat16 [8192, 512], replicated, may hold values from -0.0625 to 0.0625
- lowrank_down_weight: bfloat16 [64, 64, 8192], P(('grp', 'own')), parts along dimension 0, may hold values from -0.0625 to 0.0625
- lowrank_up_weight: bfloat16 [64, 64, 512], P(('grp', 'own')), parts along dimension 0, may hold values from -0.75 to 0.75
Outputs:
- values_out: bfloat16 [4096, 512], P(('grp', 'own')), parts along dimension 0
The draws below stay inside these ranges and needn't reach their ends.
There are 2 independent parts, one for each index of `grp`. The reference program is written for one: setup_inputs(seed, part) draws one part's arguments, and reference() takes and returns one part's arrays. A program takes and returns all parts, laid end to end along the dimension named above; an argument that names none is the same for every part. Nothing has to cross between parts.
Inputs may be any that keep to these rules, and one draw needn't show every extreme that they name: `adapter_index_rows`: among the rows of one device no adapter is named by more than 8 rows; some adapter is named by exactly 8 rows of some device. `adapter_pool_position`: each slot holds one adapter; slot s lies on the device of index s // 2 along own.
All inputs are finite; a program needn't handle non-finite values.
Results may differ from the reference program's by a relative error of at most 0.0051.
Values may be sent and summed in bfloat16 or wider, within the bound.
No kernel may reach another device: no remote copies, remote signals or barrier semaphores. Data moves between devices by JAX's collectives and lax.ppermute only.
A program may use at most 64 MiB of HBM per device.

```python
import math
import jax
import jax.numpy as jnp
import numpy as np
from jax import lax

MODEL_WIDTH = 8192
VALUE_WIDTH = 512
ADAPTER_RANK = 64
TOK_DEV = 128
ADAPTER_POOL = 32
CAP = 8
TOKENS = 2048


def block_levels(stream_key, shape, pieces, low, largest):
    level, own = 1.0, jax.random.fold_in(stream_key, 6)
    for axis_at, parts in pieces:
        heights = jnp.exp(jax.random.uniform(jax.random.fold_in(own, axis_at), (parts,), jnp.float32, low / len(pieces), largest / len(pieces)))
        level = level * jnp.repeat(heights, shape[axis_at] // parts).reshape([-1 if axis == axis_at else 1 for axis in range(len(shape))])
    return level


def deal_out(rng, own, number, rows, number_of, top, bound, lean):
    ranking = jax.random.permutation(rng, number_of)
    packed, common = portions_of(number_of, rows * top, bound, lean, True), portions_of(number_of, rows * top, bound, lean, False)
    places = jnp.arange(number_of)

    def named(lengths, offset_by):
        used = int((lengths > 0).sum())
        fixed = max(1, used // 4)
        moved = fixed + (places - fixed + offset_by * (used - fixed)) % max(1, number_of - fixed)
        return jnp.zeros((number_of,), jnp.int32).at[ranking[jnp.where(places < fixed, places, moved)]].set(jnp.asarray(lengths, jnp.int32))

    lengths = jnp.where(number % 4 == 0, named(packed, number // 4), named(common, number - number // 4 - 1))
    mixed = jax.random.permutation(jax.random.fold_in(own, 3), number_of)
    source_of, sink = mixed[0:number_of // 2 * 2:2], mixed[1:number_of // 2 * 2:2]
    margin = jnp.minimum(lengths[source_of] - 1, bound - lengths[sink]) // 2
    margin = jnp.where((source_of == ranking[0]) | (sink == ranking[0]) | (lengths[sink] == 0), 0, jnp.maximum(margin, 0))
    moved = jax.random.randint(jax.random.fold_in(own, 4), (number_of // 2,), 0, 1 << 20) % (margin + 1)
    lengths = lengths.at[source_of].add(-moved).at[sink].add(moved)
    members = jnp.searchsorted(jnp.cumsum(lengths), jnp.arange(rows * top), side="right").astype(jnp.int32)
    listing = members.reshape(top, rows).T
    listing = listing[jax.random.permutation(jax.random.fold_in(own, 1), rows)]
    offset_by = jax.random.randint(jax.random.fold_in(own, 2), (rows, 1), 0, top)
    return jnp.take_along_axis(listing, (jnp.arange(top)[None, :] + offset_by) % top, axis=1)


def portions_of(number_of, total, reach, skew, full):
    weights = [(1 << 20) // math.isqrt(rank ** skew) + 1 for rank in range(1, number_of + 1)]
    largest = reach if full else min(reach, max(-(-total // number_of), total * weights[0] // sum(weights)))
    least = 1 if total - largest >= number_of - 1 else 0
    given, spare = [largest] + [least] * (number_of - 1), total - largest - least * (number_of - 1)
    while spare > 0:
        free = [i for i in range(1, number_of) if given[i] < largest] or [i for i in range(1, number_of) if given[i] < reach]
        whole, left = sum([weights[i] for i in free]), spare
        for i in free:
            extra = min(reach - given[i], max(1, left * weights[i] // whole), spare)
            given[i] = given[i] + extra
            spare = spare - extra
    return np.array(given)


def normal_values(own_key, extent, scale, limit, split=(), held_as=jnp.bfloat16):
    values = jax.random.normal(own_key, extent, jnp.float32) * scale
    if len(split) > 0:
        values = block_levels(own_key, extent, split, -0.22, 0.18) * values
    return jnp.clip(values, min=-limit, max=limit).astype(held_as)


def setup_inputs(seed: int = 0, part: int = 0) -> dict:
    arg_keys = jax.random.split(jax.random.key(seed), 7)
    own_keys = jax.random.split(jax.random.fold_in(arg_keys[6], part), 7)
    tokens = normal_values(own_keys[0], (TOKENS, MODEL_WIDTH), 1.0, 6.0, ((0, 16),))
    adapter_index_rows_keys = jax.random.split(jax.random.fold_in(own_keys[1], 1), TOKENS // TOK_DEV)
    adapter_index_rows_turns = jax.random.permutation(jax.random.fold_in(own_keys[1], 3), TOKENS // TOK_DEV)
    adapter_index_rows = jax.vmap(lambda own, number: deal_out(jax.random.fold_in(own_keys[1], 2), own, number, TOK_DEV, ADAPTER_POOL, 1, CAP, 2))(adapter_index_rows_keys, adapter_index_rows_turns).reshape((TOKENS, 1))
    adapter_pool_position = jax.random.permutation(own_keys[2], ADAPTER_POOL).astype(jnp.int32)
    base_value_matrix = normal_values(arg_keys[3], (MODEL_WIDTH, VALUE_WIDTH), MODEL_WIDTH ** -0.5, 0.0625)
    lowrank_down_weight = normal_values(own_keys[4], (ADAPTER_POOL, ADAPTER_RANK, MODEL_WIDTH), MODEL_WIDTH ** -0.5, 0.0625, ((0, 16),))
    lowrank_up_weight = normal_values(own_keys[5], (ADAPTER_POOL, ADAPTER_RANK, VALUE_WIDTH), ADAPTER_RANK ** -0.5, 0.75, ((0, 16),))
    return dict(tokens=tokens, adapter_index_rows=adapter_index_rows, adapter_pool_position=adapter_pool_position, base_value_matrix=base_value_matrix, lowrank_down_weight=lowrank_down_weight, lowrank_up_weight=lowrank_up_weight)


def reference(tokens, adapter_index_rows, adapter_pool_position, base_value_matrix, lowrank_down_weight, lowrank_up_weight):
    slot = adapter_pool_position[adapter_index_rows[:, 0]]
    base = jnp.dot(tokens, base_value_matrix, preferred_element_type=jnp.float32)
    token_blocks = tokens.reshape(TOKENS // 32, 32, MODEL_WIDTH)
    slot_blocks = slot.reshape(TOKENS // 32, 32)

    def one_block(pair):
        rows_x, row_pool_position = pair
        down_matrix = lowrank_down_weight[row_pool_position].astype(jnp.float32)
        reduced_rows = jnp.einsum("bd,brd->br", rows_x.astype(jnp.float32), down_matrix).astype(jnp.bfloat16)
        expanded_rows = lowrank_up_weight[row_pool_position].astype(jnp.float32)
        return jnp.einsum("br,brk->bk", reduced_rows.astype(jnp.float32), expanded_rows).astype(jnp.bfloat16)

    deltas = lax.map(one_block, (token_blocks, slot_blocks)).reshape(TOKENS, VALUE_WIDTH)
    return (base + deltas.astype(jnp.float32)).astype(jnp.bfloat16)
```

```python
import jax
import jax.numpy as jnp
from jax import lax
from jax.sharding import PartitionSpec as P

LANES = 4


def select(places, rank):
    return (places[:, None] == rank[None, :]).astype(jnp.bfloat16)


def pick(hot, values):
    return jnp.dot(hot, values, preferred_element_type=jnp.float32).astype(jnp.bfloat16)


def largest_anywhere(value, mesh_shape):
    value = jnp.full((1, 128), value, jnp.int32)
    for axis, size in mesh_shape.items():
        step = 1
        while step < size:
            pairs = [(i, i ^ step) for i in range(size)]
            value = jnp.maximum(value, lax.ppermute(value, axis, pairs))
            step *= 2
    return value[0, 0]


def make_local(mesh_shape):
    owners = mesh_shape["own"]
    planes = owners // LANES

    def by_planes(shift):
        return [
            (z * LANES + lane, (z + shift) % planes * LANES + lane)
            for z in range(planes)
            for lane in range(LANES)
        ]

    def by_lane(flip):
        return [(i, i ^ flip) for i in range(owners)]

    def send(x, shift):
        return lax.ppermute(x, "own", by_planes(shift % planes))

    def local(
        tokens,
        adapter_index_rows,
        adapter_pool_position,
        base_value_matrix,
        lowrank_down_weight,
        lowrank_up_weight,
    ):
        rows, width = tokens.shape
        held, rank, _ = lowrank_down_weight.shape
        out_width = base_value_matrix.shape[1]
        total = adapter_pool_position.shape[0]
        most = max(2, 2 * rows // total)
        cap = min(rows, LANES * held * most)
        first = cap // 2
        second = cap // 4
        third = cap - first - second
        levels = sorted({second * k // 8 for k in range(9)})
        shifts = sorted(range(1, planes), key=lambda s: -min(s, planes - s))

        me = lax.axis_index("own")
        plane, lane = me // LANES, me % LANES

        down = [lowrank_down_weight.reshape(held * rank, width)]
        up = [lowrank_up_weight.reshape(held * rank, out_width)]
        for flip in (1, 2):
            down = down + [lax.ppermute(x, "own", by_lane(flip)) for x in down]
            up = up + [lax.ppermute(x, "own", by_lane(flip)) for x in up]

        chosen = adapter_index_rows[:, 0]
        table = jnp.arange(total, dtype=jnp.int32)
        slot = jnp.sum(
            jnp.where(chosen[:, None] == table[None, :], adapter_pool_position[None, :], 0), axis=1
        )
        owner = slot // held
        shift_of = (owner // LANES - plane + planes) % planes
        column = ((owner % LANES) ^ lane) * held + slot % held
        places = jnp.arange(rows, dtype=jnp.int32)
        earlier = (shift_of[:, None] == shift_of[None, :]) & (places[None, :] < places[:, None])
        within = jnp.sum(earlier.astype(jnp.int32), axis=1)
        order = {s: jnp.where(shift_of == s, within, -1) for s in shifts}
        needed = jnp.max(jnp.where(shift_of > 0, within + 1, 0))
        needed = largest_anywhere(needed, mesh_shape)

        def hot(s, start, count):
            return select(jnp.arange(start, start + count, dtype=jnp.int32), order[s])

        arrived_column = {
            s: send(
                jnp.sum(
                    jnp.where(
                        jnp.arange(cap, dtype=jnp.int32)[:, None] == order[s][None, :],
                        column[None, :] + 1,
                        0,
                    ),
                    axis=1,
                )[None, :]
                - 1,
                s,
            )[0]
            for s in shifts
        }
        sent_first = {s: send(pick(hot(s, 0, first), tokens), s) for s in shifts}

        base = jnp.dot(tokens, base_value_matrix, preferred_element_type=jnp.float32)

        def level_branch(count):
            def branch(tokens, orders):
                out = []
                for s, o in zip(shifts, orders):
                    places = jnp.arange(first, first + count, dtype=jnp.int32)
                    if count:
                        got = send(pick(select(places, o), tokens), s)
                        out.append(jnp.pad(got, ((0, second - count), (0, 0))))
                    else:
                        out.append(jnp.zeros((second, width), tokens.dtype))
                return tuple(out)

            return branch

        level = jnp.sum((needed - first > jnp.array(levels[:-1])).astype(jnp.int32))
        sent_second = lax.switch(
            level,
            [level_branch(c) for c in levels],
            tokens,
            tuple(order[s] for s in shifts),
        )
        sent_second = dict(zip(shifts, sent_second))

        def adapters(x, columns):
            shrunk = jnp.concatenate(
                [
                    lax.dot_general(
                        x, w, (((1,), (1,)), ((), ())), preferred_element_type=jnp.float32
                    )
                    for w in down
                ],
                axis=1,
            )
            named = jnp.arange(shrunk.shape[1], dtype=jnp.int32)[None, :] // rank
            shrunk = jnp.where(named == columns[:, None], shrunk, 0).astype(jnp.bfloat16)
            return jnp.dot(
                shrunk, jnp.concatenate(up, axis=0), preferred_element_type=jnp.float32
            ).astype(jnp.bfloat16)

        both = first + second
        arrived = jnp.concatenate(
            [tokens] + [x for s in shifts for x in (sent_first[s], sent_second[s])], axis=0
        )
        arrived_columns = jnp.concatenate(
            [jnp.where(shift_of == 0, column, -1)] + [arrived_column[s][:both] for s in shifts]
        )
        computed = adapters(arrived, arrived_columns)
        own_delta = computed[:rows].astype(jnp.float32)
        returned = [
            send(computed[rows + i * both : rows + (i + 1) * both], -s)
            for i, s in enumerate(shifts)
        ]
        delta = own_delta + jnp.dot(
            jnp.concatenate([hot(s, 0, both) for s in shifts], axis=0).T,
            jnp.concatenate(returned, axis=0),
            preferred_element_type=jnp.float32,
        )

        def rest(tokens):
            sent = [send(pick(hot(s, both, third), tokens), s) for s in shifts]
            done = adapters(
                jnp.concatenate(sent, axis=0),
                jnp.concatenate([arrived_column[s][both:] for s in shifts]),
            )
            back = [send(done[i * third : (i + 1) * third], -s) for i, s in enumerate(shifts)]
            return jnp.dot(
                jnp.concatenate([hot(s, both, third) for s in shifts], axis=0).T,
                jnp.concatenate(back, axis=0),
                preferred_element_type=jnp.float32,
            )

        delta = delta + lax.cond(
            needed > both, rest, lambda x: jnp.zeros((rows, out_width), jnp.float32), tokens
        )
        return (base + delta).astype(jnp.bfloat16)

    return local


def solution(mesh):
    in_specs = (
        P(("grp", "own"), None),
        P(("grp", "own"), None),
        P("grp"),
        P(),
        P(("grp", "own"), None, None),
        P(("grp", "own"), None, None),
    )
    out_specs = P(("grp", "own"), None)
    return jax.shard_map(
        make_local(dict(mesh.shape)),
        mesh=mesh,
        in_specs=in_specs,
        out_specs=out_specs,
        check_vma=False,
    )
```

```python
import functools

import jax
import jax.numpy as jnp
from jax import lax
from jax.experimental import pallas as pl
from jax.experimental.pallas import tpu as pltpu
from jax.sharding import PartitionSpec as P

LANES = 4
MATMUL_T = (((1,), (1,)), ((), ()))
PARAMS = pltpu.CompilerParams(vmem_limit_bytes=40 * 1024 * 1024)


def tile_of(width):
    return next(t for t in (1024, 512, 256, 128, width) if width % t == 0)


def count_body(starts, levels, place_ref, mine_ref, mate_ref, out_ref):
    mine, mate = mine_ref[...], mate_ref[...]
    chip_rows = jnp.zeros((1, 1), jnp.int32)
    device_rows = jnp.zeros((1, 1), jnp.int32)
    for p, (low, high) in enumerate(starts):
        counts = []
        for packed in (mine, mate):
            here = (packed >= low) & (packed < high) & (place_ref[1] != p)
            counts.append(
                jnp.sum(jnp.where(here, 1.0, 0.0), axis=1, keepdims=True).astype(jnp.int32)
            )
        chip_rows = jnp.maximum(chip_rows, counts[0] + counts[1])
        device_rows = jnp.maximum(device_rows, jnp.maximum(*counts))
    level = jnp.zeros((1, 1), jnp.int32)
    for chip_cap, device_cap in levels[:-1]:
        level = level + ((chip_rows > chip_cap) | (device_rows > device_cap)).astype(jnp.int32)
    out_ref[0:1, :] = mine
    out_ref[1:2, :] = mate
    out_ref[2:3, :] = jnp.broadcast_to(level, mine.shape)


def count(place, mine, mate, starts, levels):
    return pl.pallas_call(
        functools.partial(count_body, starts, levels),
        out_shape=jax.ShapeDtypeStruct((3, mine.shape[1]), jnp.int32),
        in_specs=[
            pl.BlockSpec(memory_space=pltpu.SMEM),
            pl.BlockSpec(memory_space=pltpu.VMEM),
            pl.BlockSpec(memory_space=pltpu.VMEM),
        ],
        out_specs=pl.BlockSpec(memory_space=pltpu.VMEM),
    )(place, mine, mate)


def pack_body(shifts, planes, place_ref, goes_ref, within_ref, kept_ref, mate_ref, *outs):
    core, plane = place_ref[0], place_ref[1]
    size = outs[0].shape[0]
    spots = lax.broadcasted_iota(jnp.int32, (size, kept_ref.shape[0]), 0)
    for s, out in zip(shifts, outs):
        to = lax.rem(plane + s, planes)
        packed = jnp.zeros(out.shape, jnp.float32)
        for row, rows_ref in enumerate((kept_ref, mate_ref)):
            within = within_ref[row : row + 1, :]
            spot = jnp.where(core == row, within, size - 1 - within)
            spot = jnp.where(goes_ref[row : row + 1, :] == to, spot, -1)
            hot = jnp.where(spots == spot, 1.0, 0.0).astype(jnp.bfloat16)
            packed += jnp.dot(hot, rows_ref[...], preferred_element_type=jnp.float32)
        out[...] = packed.astype(out.dtype)


def pack(place, goes_to, within, tokens, mate, size, shifts, planes):
    rows, half = mate.shape
    tile = tile_of(half)
    steps = half // tile
    whole = lambda a: pl.BlockSpec(a.shape, lambda k, place: (0, 0))
    strip = pl.BlockSpec((rows, tile), lambda k, place: (0, k))
    return pl.pallas_call(
        functools.partial(pack_body, shifts, planes),
        grid_spec=pltpu.PrefetchScalarGridSpec(
            num_scalar_prefetch=1,
            grid=(steps,),
            in_specs=[
                whole(goes_to),
                whole(within),
                pl.BlockSpec((rows, tile), lambda k, place: (0, place[0] * steps + k)),
                strip,
            ],
            out_specs=[pl.BlockSpec((size, tile), lambda k, place: (0, k)) for _ in shifts],
        ),
        out_shape=[jax.ShapeDtypeStruct((size, half), mate.dtype) for _ in shifts],
        compiler_params=PARAMS,
        cost_estimate=pl.CostEstimate(
            flops=4 * len(shifts) * size * rows * half,
            bytes_accessed=2 * half * (2 * rows + len(shifts) * size),
            transcendentals=0,
        ),
    )(place, goes_to, within, tokens, mate)


def shrink_body(number, maps, rank, place_ref, *refs):
    xs, ws = refs[:number], refs[number : number + maps]
    column, out, total = refs[number + maps :]
    step = pl.program_id(0)
    rows = jnp.concatenate([x[...] for x in xs], axis=0)
    weights = jnp.concatenate([w[...] for w in ws], axis=0)
    part = lax.dot_general(rows, weights, MATMUL_T, preferred_element_type=jnp.float32)

    @pl.when(step == 0)
    def _():
        total[...] = part

    @pl.when(step != 0)
    def _():
        total[...] += part

    @pl.when(step == pl.num_programs(0) - 1)
    def _():
        lanes = lax.broadcasted_iota(jnp.int32, total.shape, 1)
        low = column[...] * rank
        picked = jnp.where((lanes >= low) & (lanes < low + rank), total[...], 0.0)
        folded = picked[:, :rank]
        for q in range(1, total.shape[1] // rank):
            folded = folded + picked[:, q * rank : (q + 1) * rank]
        out[...] = folded


def shrink(place, xs, ws, column, rank):
    half = min(x.shape[1] for x in xs)
    tile = tile_of(half)
    steps = half // tile
    rows, named = sum(x.shape[0] for x in xs), sum(w.shape[0] for w in ws)

    def strip(a):
        if a.shape[1] == half:
            return pl.BlockSpec((a.shape[0], tile), lambda k, place: (0, k))
        return pl.BlockSpec((a.shape[0], tile), lambda k, place: (0, place[0] * steps + k))

    return pl.pallas_call(
        functools.partial(shrink_body, len(xs), len(ws), rank),
        grid_spec=pltpu.PrefetchScalarGridSpec(
            num_scalar_prefetch=1,
            grid=(steps,),
            in_specs=[strip(x) for x in xs]
            + [strip(w) for w in ws]
            + [pl.BlockSpec(column.shape, lambda k, place: (0, 0))],
            out_specs=pl.BlockSpec((rows, rank), lambda k, place: (0, 0)),
            scratch_shapes=[pltpu.VMEM((rows, named), jnp.float32)],
        ),
        out_shape=jax.ShapeDtypeStruct((rows, rank), jnp.float32),
        compiler_params=PARAMS,
        cost_estimate=pl.CostEstimate(
            flops=2 * rows * named * half,
            bytes_accessed=2 * half * (rows + named),
            transcendentals=0,
        ),
    )(place, *xs, *ws, column)


def expand_body(chip_cap, device_cap, place_ref, one_ref, two_ref, column_ref, up_ref, *outs):
    rank, named = one_ref.shape[1], up_ref.shape[0]
    row = lax.broadcasted_iota(jnp.int32, (rank, named), 0)
    lane = lax.broadcasted_iota(jnp.int32, (rank, named), 1)
    spread = jnp.zeros((rank, named), jnp.float32)
    for q in range(named // rank):
        spread = jnp.where(lane == row + q * rank, 1.0, spread)
    spread = spread.astype(jnp.bfloat16)
    lanes = lax.broadcasted_iota(jnp.int32, (device_cap, named), 1)
    for i, out in enumerate(outs):
        front, back = i * chip_cap, (i + 1) * chip_cap - device_cap

        def window(ref):
            a, b = ref[front : front + device_cap, :], ref[back : back + device_cap, :]
            return jnp.where(place_ref[0] == 0, a, b)

        shrunk = (window(one_ref) + window(two_ref)).astype(jnp.bfloat16)
        low = window(column_ref) * rank
        wide = jnp.dot(shrunk, spread, preferred_element_type=jnp.float32)
        wide = jnp.where((lanes >= low) & (lanes < low + rank), wide, 0.0).astype(jnp.bfloat16)
        out[...] = jnp.dot(wide, up_ref[...], preferred_element_type=jnp.float32).astype(
            out.dtype
        )


def expand(place, one, two, column, up, number, device_cap):
    chip_cap = one.shape[0] // number
    return pl.pallas_call(
        functools.partial(expand_body, chip_cap, device_cap),
        in_specs=[pl.BlockSpec(memory_space=pltpu.SMEM)]
        + [pl.BlockSpec(memory_space=pltpu.VMEM) for _ in range(4)],
        out_specs=[pl.BlockSpec(memory_space=pltpu.VMEM) for _ in range(number)],
        out_shape=[jax.ShapeDtypeStruct((device_cap, up.shape[1]), up.dtype)] * number,
        compiler_params=PARAMS,
        cost_estimate=pl.CostEstimate(
            flops=2 * number * device_cap * up.shape[0] * up.shape[1],
            bytes_accessed=2 * up.size + 8 * one.size,
            transcendentals=0,
        ),
    )(place, one, two, column, up)


def make_local(mesh_shape):
    owners, groups = mesh_shape["own"], mesh_shape["grp"]
    planes = owners // LANES

    def send(x, shift):
        pairs = [
            (z * LANES + lane, (z + shift) % planes * LANES + lane)
            for z in range(planes)
            for lane in range(LANES)
        ]
        return lax.ppermute(x, "own", pairs)

    def swap(x, flip):
        return lax.ppermute(x, "own", [(i, i ^ flip) for i in range(owners)])

    def swap_group(x, group, flip):
        pairs = [
            (g * owners + i, (g + group) % groups * owners + (i ^ flip))
            for g in range(groups)
            for i in range(owners)
        ]
        return lax.ppermute(x, ("grp", "own"), pairs)

    def local(
        tokens,
        adapter_index_rows,
        adapter_pool_position,
        base_value_matrix,
        lowrank_down_weight,
        lowrank_up_weight,
    ):
        rows, width = tokens.shape
        held, rank, _ = lowrank_down_weight.shape
        out_width = base_value_matrix.shape[1]
        total = adapter_pool_position.shape[0]
        most = max(2, 2 * rows // total)
        cap = min(rows, LANES * held * most)
        levels = [(2 * cap * k // 16, cap * 3 // 4) for k in (10, 11, 12)] + [(2 * cap, cap)]
        shifts = sorted(range(1, planes), key=lambda s: -min(s, planes - s))
        half = width // 2

        me = lax.axis_index("own")
        plane, lane, core = me // LANES, me % LANES, me % 2
        place = jnp.stack([core, plane]).astype(jnp.int32)

        chosen = adapter_index_rows[:, 0]
        table = jnp.arange(total, dtype=jnp.int32)
        slot = jnp.sum(
            jnp.where(chosen[:, None] == table[None, :], adapter_pool_position[None, :], 0), axis=1
        )
        goes_to = slot // (held * LANES)
        places = jnp.arange(rows, dtype=jnp.int32)
        earlier = (goes_to[:, None] == goes_to[None, :]) & (places[None, :] < places[:, None])
        within = jnp.sum(earlier.astype(jnp.int32), axis=1)
        mine = (slot * rows + within)[None, :]
        mate = swap(mine, 1)

        mate, wide_tokens, wide_down, up = lax.optimization_barrier(
            (
                mate,
                tokens,
                lowrank_down_weight.reshape(held * rank, width),
                lowrank_up_weight.reshape(held * rank, out_width),
            )
        )
        other_half = lambda x: lax.dynamic_slice_in_dim(x, (1 - core) * half, half, axis=1)
        mate_tokens = swap(other_half(wide_tokens), 1)
        mate_down = swap(other_half(wide_down), 1)
        kept_down = lax.dynamic_slice_in_dim(wide_down, core * half, half, axis=1)
        up = jnp.concatenate([up, swap(up, 1)], axis=0)
        up = jnp.concatenate([up, swap(up, 2)], axis=0)

        span = rows * held * LANES
        starts = [(p * span, (p + 1) * span) for p in range(planes)]
        payload = count(place, mine, mate, starts, levels)
        info, level = payload[:2], payload[2:]
        infos = {s: send(payload, s) for s in shifts}
        for s in shifts:
            level = jnp.maximum(level, infos[s][2:])
        others = [
            swap_group(level, g, flip)
            for g in range(groups)
            for flip in (0, 2)
            if g or flip
        ]
        for other in others:
            level = jnp.maximum(level, other)
        level = level[0, 0]
        goes_to, within = info // span, info % rows

        def column_of(packed):
            slot = packed // rows
            return ((slot // held) % LANES ^ lane) * held + slot % held

        def at_level(chip_cap, device_cap):
            def spot_of(packed, size):
                from_front = packed % rows
                return jnp.where(
                    jnp.stack([core, 1 - core])[: packed.shape[0], None] == 0,
                    from_front,
                    size - 1 - from_front,
                )

            def branch(
                tokens, mate_tokens, info, goes_to, within, infos, kept_down, mate_down, up, matrix
            ):
                packed = pack(
                    place, goes_to, within, tokens, mate_tokens, chip_cap, shifts, planes
                )
                arrived = [send(x, s) for x, s in zip(packed, shifts)]
                down = [kept_down, mate_down]
                down = down + [swap(x, 2) for x in down]

                base = jnp.dot(tokens, matrix, preferred_element_type=jnp.float32)
                spots = jnp.arange(chip_cap, dtype=jnp.int32)
                columns = []
                for got in infos:
                    got = got[:2]
                    spot = jnp.where(got // span == plane, spot_of(got, chip_cap), -1)
                    columns.append(
                        jnp.sum(
                            jnp.where(
                                spots[:, None] == spot.reshape(1, -1),
                                column_of(got).reshape(1, -1) + 1,
                                0,
                            ),
                            axis=1,
                            keepdims=True,
                        )
                        - 1
                    )
                columns = jnp.concatenate(columns, axis=0)
                stays = jnp.where(goes_to == plane, column_of(info), -1).reshape(-1, 1)
                own = shrink(place, [tokens, mate_tokens], down, stays, rank)
                (own_delta,) = expand(
                    place, own[:rows], swap(own[rows:], 1), stays[:rows], up, 1, rows
                )
                out = base + own_delta.astype(jnp.float32)
                arrived, columns, out = lax.optimization_barrier((arrived, columns, out))

                sums = shrink(place, arrived, down, columns, rank)
                deltas = expand(place, sums, swap(sums, 1), columns, up, len(shifts), device_cap)
                home = [send(x, -s) for x, s in zip(deltas, shifts)]
                spots = jnp.arange(device_cap, dtype=jnp.int32)
                for s, back in zip(shifts, home):
                    spot = spot_of(info[:1], device_cap)
                    spot = jnp.where(goes_to[:1] == (plane + s) % planes, spot, -1)
                    hot = (spots[None, :] == spot.reshape(-1, 1)).astype(jnp.bfloat16)
                    out = out + jnp.dot(hot, back, preferred_element_type=jnp.float32)
                return out.astype(jnp.bfloat16)

            return branch

        return lax.switch(
            level,
            [at_level(*sizes) for sizes in levels],
            tokens,
            mate_tokens,
            info,
            goes_to,
            within,
            [infos[s] for s in shifts],
            kept_down,
            mate_down,
            up,
            base_value_matrix,
        )

    return local


def solution(mesh):
    in_specs = (
        P(("grp", "own"), None),
        P(("grp", "own"), None),
        P("grp"),
        P(),
        P(("grp", "own"), None, None),
        P(("grp", "own"), None, None),
    )
    out_specs = P(("grp", "own"), None)
    return jax.shard_map(
        make_local(dict(mesh.shape)),
        mesh=mesh,
        in_specs=in_specs,
        out_specs=out_specs,
        check_vma=False,
    )
```

```python
import functools

import jax
import jax.numpy as jnp
from jax import lax
from jax.experimental import pallas as pl
from jax.experimental.pallas import tpu as pltpu
from jax.sharding import PartitionSpec as P

LANES = 4
MATMUL_T = (((1,), (1,)), ((), ()))
PARAMS = pltpu.CompilerParams(vmem_limit_bytes=40 * 1024 * 1024)


def tile_of(width):
    return next(t for t in (2048, 1024, 512, 256, 128, width) if width % t == 0)


def level_body(starts, levels, first, place_ref, mine_ref, mate_ref, out_ref):
    mine, mate = mine_ref[...], mate_ref[...]
    planes = mine.shape[0]
    row = lax.broadcasted_iota(jnp.int32, (planes, 1), 0)
    source = jnp.bitwise_xor(row, place_ref[1])
    level = jnp.zeros((planes, 1), jnp.int32)
    for p, (low, high) in enumerate(starts):
        counts = []
        for packed in (mine, mate):
            here = jnp.where((packed >= low) & (packed < high), 1.0, 0.0)
            number = jnp.sum(here, axis=1, keepdims=True).astype(jnp.int32) - first
            counts.append(jnp.maximum(jnp.where(source == p, 0, number), 0))
        chip_rows, device_rows = counts[0] + counts[1], jnp.maximum(*counts)
        needed = jnp.zeros((planes, 1), jnp.int32)
        for chip_cap, device_cap in levels[:-1]:
            needed += jnp.where((chip_rows > chip_cap) | (device_rows > device_cap), 1, 0)
        level = jnp.maximum(level, needed)
    highest = level[0:1, :]
    for k in range(1, planes):
        highest = jnp.maximum(highest, level[k : k + 1, :])
    out_ref[...] = jnp.broadcast_to(highest, out_ref.shape)


def level_of(place, mine, mate, starts, levels, first):
    return pl.pallas_call(
        functools.partial(level_body, starts, levels, first),
        out_shape=jax.ShapeDtypeStruct((1, mine.shape[1]), jnp.int32),
        in_specs=[
            pl.BlockSpec(memory_space=pltpu.SMEM),
            pl.BlockSpec(memory_space=pltpu.VMEM),
            pl.BlockSpec(memory_space=pltpu.VMEM),
        ],
        out_specs=pl.BlockSpec(memory_space=pltpu.VMEM),
    )(place, mine, mate)


def pack_body(flips, number, start, place_ref, goes_ref, within_ref, *refs):
    core, plane, back = place_ref[0], place_ref[1], place_ref[2]
    values, outs, hot = refs[:number], refs[number:-1], refs[-1]
    size, rows = outs[0].shape[0], values[0].shape[0]

    @pl.when(pl.program_id(0) == 0)
    def _():
        spots = lax.broadcasted_iota(jnp.int32, (size, rows), 0)
        parts = []
        for flip in flips:
            to = jnp.bitwise_xor(plane, flip)
            sides = []
            for row in range(number):
                within = within_ref[row : row + 1, :] - start
                spot = within if number == 1 else jnp.where(core == row, within, back - 1 - within)
                named = (goes_ref[row : row + 1, :] == to) & (within >= 0) & (within < size)
                sides.append(jnp.where(spots == jnp.where(named, spot, -1), 1.0, 0.0))
            parts.append(jnp.concatenate(sides, axis=1))
        hot[...] = jnp.concatenate(parts, axis=0).astype(hot.dtype)

    rows_of_chip = jnp.concatenate([v[...] for v in values], axis=0)
    packed = jnp.dot(hot[...], rows_of_chip, preferred_element_type=jnp.float32)
    for i, out in enumerate(outs):
        out[...] = packed[i * size : (i + 1) * size, :].astype(out.dtype)


def pack(place, goes_to, within, values, start, size, flips):
    number, (rows, width) = len(values), values[0].shape
    width = width // number
    tile = tile_of(width)
    steps = width // tile
    whole = lambda a: pl.BlockSpec(a.shape, lambda k, place: (0, 0))
    strip = pl.BlockSpec(
        (rows, tile), lambda k, place: (0, k if number == 1 else place[0] * steps + k)
    )
    return pl.pallas_call(
        functools.partial(pack_body, flips, number, start),
        grid_spec=pltpu.PrefetchScalarGridSpec(
            num_scalar_prefetch=1,
            grid=(steps,),
            in_specs=[whole(goes_to), whole(within)] + [strip] * number,
            out_specs=[pl.BlockSpec((size, tile), lambda k, place: (0, k)) for _ in flips],
            scratch_shapes=[pltpu.VMEM((len(flips) * size, number * rows), values[0].dtype)],
        ),
        out_shape=[jax.ShapeDtypeStruct((size, width), values[0].dtype) for _ in flips],
        compiler_params=PARAMS,
        cost_estimate=pl.CostEstimate(
            flops=2 * len(flips) * size * number * rows * width,
            bytes_accessed=2 * width * (number * rows + len(flips) * size),
            transcendentals=0,
        ),
    )(place, goes_to, within, *values)


def shrink_body(number, maps, rank, start, place_ref, *refs):
    xs, ws = refs[:number], refs[number : number + maps]
    column, out, total = refs[number + maps :]
    step = pl.program_id(0)
    rows = jnp.concatenate([x[...] for x in xs], axis=0)
    weights = jnp.concatenate([w[...] for w in ws], axis=0)
    part = lax.dot_general(rows, weights, MATMUL_T, preferred_element_type=jnp.float32)

    @pl.when(step == 0)
    def _():
        total[...] = part

    @pl.when(step != 0)
    def _():
        total[...] += part

    @pl.when(step == pl.num_programs(0) - 1)
    def _():
        lanes = lax.broadcasted_iota(jnp.int32, total.shape, 1)
        low = (column[...] - start) * rank
        picked = jnp.where((lanes >= low) & (lanes < low + rank), total[...], 0.0)
        folded = picked[:, :rank]
        for q in range(1, total.shape[1] // rank):
            folded = folded + picked[:, q * rank : (q + 1) * rank]
        out[...] = folded


def shrink(place, xs, ws, column, rank, start=0):
    half = ws[0].shape[1]
    tile = tile_of(half)
    steps = half // tile
    rows, named = sum(x.shape[0] for x in xs), sum(w.shape[0] for w in ws)

    def strip(a):
        if a.shape[1] == half:
            return pl.BlockSpec((a.shape[0], tile), lambda k, place: (0, k))
        return pl.BlockSpec((a.shape[0], tile), lambda k, place: (0, place[0] * steps + k))

    return pl.pallas_call(
        functools.partial(shrink_body, len(xs), len(ws), rank, start),
        grid_spec=pltpu.PrefetchScalarGridSpec(
            num_scalar_prefetch=1,
            grid=(steps,),
            in_specs=[strip(x) for x in xs]
            + [strip(w) for w in ws]
            + [pl.BlockSpec(column.shape, lambda k, place: (0, 0))],
            out_specs=pl.BlockSpec((rows, rank), lambda k, place: (0, 0)),
            scratch_shapes=[pltpu.VMEM((rows, named), jnp.float32)],
        ),
        out_shape=jax.ShapeDtypeStruct((rows, rank), jnp.float32),
        compiler_params=PARAMS,
        cost_estimate=pl.CostEstimate(
            flops=2 * rows * named * half,
            bytes_accessed=2 * half * (rows + named),
            transcendentals=0,
        ),
    )(place, *xs, *ws, column)


def expand_body(chip_cap, device_cap, number, place_ref, one_ref, two_ref, column_ref, up_ref, *refs):
    given, outs = (refs[0], refs[1:]) if len(refs) > number else (None, refs)
    rank, named = one_ref.shape[1], up_ref.shape[0]
    row = lax.broadcasted_iota(jnp.int32, (rank, named), 0)
    lane = lax.broadcasted_iota(jnp.int32, (rank, named), 1)
    spread = jnp.zeros((rank, named), jnp.float32)
    for q in range(named // rank):
        spread = jnp.where(lane == row + q * rank, 1.0, spread)
    spread = spread.astype(jnp.bfloat16)

    def window(ref):
        parts = []
        for i in range(number):
            front, back = i * chip_cap, (i + 1) * chip_cap - device_cap
            a, b = ref[front : front + device_cap, :], ref[back : back + device_cap, :]
            parts.append(a if front == back else jnp.where(place_ref[0] == 0, a, b))
        return jnp.concatenate(parts, axis=0)

    shrunk = (window(one_ref) + window(two_ref)).astype(jnp.bfloat16)
    low = window(column_ref) * rank
    lanes = lax.broadcasted_iota(jnp.int32, (number * device_cap, named), 1)
    wide = jnp.dot(shrunk, spread, preferred_element_type=jnp.float32)
    wide = jnp.where((lanes >= low) & (lanes < low + rank), wide, 0.0).astype(jnp.bfloat16)
    delta = jnp.dot(wide, up_ref[...], preferred_element_type=jnp.float32)
    for i, out in enumerate(outs):
        mine = delta[i * device_cap : (i + 1) * device_cap, :].astype(out.dtype)
        if given is None:
            out[...] = mine
        else:
            first = out.shape[0] - device_cap
            out[...] = jnp.concatenate([given[i * first : (i + 1) * first, :], mine], axis=0)


def expand(place, one, two, column, up, number, device_cap, given=None):
    chip_cap = one.shape[0] // number
    rows = device_cap + (0 if given is None else given.shape[0] // number)
    operands = [place, one, two, column, up] + ([] if given is None else [given])
    return pl.pallas_call(
        functools.partial(expand_body, chip_cap, device_cap, number),
        in_specs=[pl.BlockSpec(memory_space=pltpu.SMEM)]
        + [pl.BlockSpec(memory_space=pltpu.VMEM) for _ in operands[1:]],
        out_specs=[pl.BlockSpec(memory_space=pltpu.VMEM) for _ in range(number)],
        out_shape=[jax.ShapeDtypeStruct((rows, up.shape[1]), up.dtype)] * number,
        compiler_params=PARAMS,
        cost_estimate=pl.CostEstimate(
            flops=2 * number * device_cap * up.shape[0] * up.shape[1],
            bytes_accessed=2 * up.size + 8 * one.size,
            transcendentals=0,
        ),
    )(*operands)


def make_local(mesh_shape):
    owners, groups = mesh_shape["own"], mesh_shape["grp"]
    planes = owners // LANES

    def flipped(x, axis, flip):
        size = mesh_shape[axis]
        return lax.ppermute(x, axis, [(i, i ^ flip) for i in range(size)])

    def swap(x, flip):
        return flipped(x, "own", flip)

    def send(x, flip):
        return flipped(x, "own", flip * LANES)

    def local(
        tokens,
        adapter_index_rows,
        adapter_pool_position,
        base_value_matrix,
        lowrank_down_weight,
        lowrank_up_weight,
    ):
        rows, width = tokens.shape
        held, rank, _ = lowrank_down_weight.shape
        out_width = base_value_matrix.shape[1]
        total = adapter_pool_position.shape[0]
        most = max(2, 2 * rows // total)
        cap = min(rows, LANES * held * most)
        first = cap // 4
        levels = [(2 * cap * k // 16 - 2 * first, cap * 3 // 4 - first) for k in (10, 11, 12)]
        levels = levels + [(2 * cap - 2 * first, cap - first)]
        flips = sorted(range(1, planes), key=lambda k: -k)
        half = width // 2

        me = lax.axis_index("own")
        plane, lane, core = me // LANES, me % LANES, me % 2
        place = jnp.stack([core, plane, jnp.zeros_like(core)]).astype(jnp.int32)

        chosen = adapter_index_rows[:, 0]
        table = jnp.arange(total, dtype=jnp.int32)
        slot = jnp.sum(
            jnp.where(chosen[:, None] == table[None, :], adapter_pool_position[None, :], 0), axis=1
        )
        goes_to = slot // (held * LANES)
        places = jnp.arange(rows, dtype=jnp.int32)
        earlier = (goes_to[:, None] == goes_to[None, :]) & (places[None, :] < places[:, None])
        within = jnp.sum(earlier.astype(jnp.int32), axis=1)
        mine = (slot * rows + within)[None, :]

        down = lowrank_down_weight.reshape(held * rank, width)
        up = lowrank_up_weight.reshape(held * rank, out_width)
        half_of = lambda x, c: lax.dynamic_slice_in_dim(x, c * half, half, axis=1)
        mate_tokens, mate_down, mate_up = swap(tokens, 1), swap(down, 1), swap(up, 1)
        kept_down = half_of(down, core)
        far_down = swap(kept_down, 2)

        infos, step = mine, 1
        while step < planes:
            infos = jnp.concatenate([infos, send(infos, step)], axis=0)
            step *= 2
        first_rows = pack(place, goes_to[None, :], within[None, :], [tokens], 0, first, flips)
        infos, first_rows, mate_tokens, mate_down, mate_up = lax.optimization_barrier(
            (infos, first_rows, mate_tokens, mate_down, mate_up)
        )
        first_arrived = [send(x, k) for x, k in zip(first_rows, flips)]
        mate_infos = swap(infos, 1)
        span = rows * held * LANES
        starts = [(p * span, (p + 1) * span) for p in range(planes)]
        level = level_of(place, infos, mate_infos, starts, levels, first)
        level = jnp.maximum(level, swap(level, 2))
        step = 1
        while step < groups:
            level = jnp.maximum(level, flipped(level, "grp", step))
            step *= 2
        level = level[0, 0]
        infos = jnp.stack([infos, mate_infos], axis=1)
        info = infos[0]
        goes_to, within = info // span, info % rows
        near_down = lax.optimization_barrier(half_of(mate_down, core))

        def column_of(packed):
            slot = packed // rows
            return ((slot // held) % LANES ^ lane) * held + slot % held

        def at_level(chip_cap, device_cap):
            home_core = jnp.stack([core, 1 - core])[:, None]

            def spot_of(packed, size):
                ahead = packed % rows - first
                spot = jnp.where(home_core[: packed.shape[0]] == 0, ahead, size - 1 - ahead)
                return jnp.where(ahead >= 0, spot, -1)

            def named_by(spots, spot, column):
                hot = spots[:, None] == spot.reshape(1, -1)
                return jnp.sum(jnp.where(hot, column.reshape(1, -1) + 1, 0), 1, keepdims=True) - 1

            def branch(
                tokens,
                mate_tokens,
                info,
                goes_to,
                within,
                infos,
                first_arrived,
                kept_down,
                near_down,
                far_down,
                up,
                mate_up,
                matrix,
            ):
                packed = pack(
                    jnp.stack([core, plane, jnp.full_like(core, chip_cap)]),
                    goes_to,
                    within,
                    [tokens, mate_tokens],
                    first,
                    chip_cap,
                    flips,
                )
                packed, first_arrived, up, tokens, infos = lax.optimization_barrier(
                    (packed, first_arrived, up, tokens, infos)
                )
                arrived = [send(x, k) for x, k in zip(packed, flips)]
                last_down = swap(near_down, 2)
                down = [kept_down, near_down, far_down, last_down]
                up = jnp.concatenate([up, mate_up], axis=0)
                up = jnp.concatenate([up, swap(up, 2)], axis=0)
                first_mine = jnp.concatenate(first_arrived, axis=0)
                first_mate = swap(first_mine, 1)

                base = jnp.dot(tokens, matrix, preferred_element_type=jnp.float32)
                columns, first_columns = [], [[], []]
                for k in flips:
                    got = infos[k]
                    here = got // span == plane
                    columns.append(
                        named_by(
                            jnp.arange(chip_cap, dtype=jnp.int32),
                            jnp.where(here, spot_of(got, chip_cap), -1),
                            column_of(got),
                        )
                    )
                    for row in range(2):
                        first_columns[row].append(
                            named_by(
                                jnp.arange(first, dtype=jnp.int32),
                                jnp.where(here, got % rows, -1)[row],
                                column_of(got)[row],
                            )
                        )
                columns = jnp.concatenate(columns, axis=0)
                stays = jnp.where(goes_to == plane, column_of(info), -1)[:, :, None]
                own_columns = jnp.concatenate([stays[0]] + first_columns[0], axis=0)
                mate_columns = jnp.concatenate([stays[1]] + first_columns[1], axis=0)
                held_rows = own_columns.shape[0]
                rows_here = [tokens, first_mine, mate_tokens, first_mate]
                columns_here = jnp.concatenate([own_columns, mate_columns], axis=0)
                sums = shrink(place, rows_here, down[:3], columns_here, rank)
                sums = sums + shrink(place, rows_here, down[3:], columns_here, rank, 3 * held)
                (delta,) = expand(
                    place,
                    sums[:held_rows],
                    swap(sums[held_rows:], 1),
                    own_columns,
                    up,
                    1,
                    held_rows,
                )
                out = base + delta[:rows].astype(jnp.float32)
                arrived, columns, out, first_delta = lax.optimization_barrier(
                    (arrived, columns, out, delta[rows:])
                )

                sums = shrink(place, arrived, down, columns, rank)
                deltas = expand(
                    place,
                    sums,
                    swap(sums, 1),
                    columns,
                    up,
                    len(flips),
                    device_cap,
                    first_delta,
                )
                home = [send(x, k) for x, k in zip(deltas, flips)]
                spots = jnp.arange(first + device_cap, dtype=jnp.int32)
                for k, back in zip(flips, home):
                    ahead = info[:1] % rows
                    rest = spot_of(info[:1], device_cap) + first
                    spot = jnp.where(ahead < first, ahead, rest)
                    spot = jnp.where(goes_to[:1] == plane ^ k, spot, -1)
                    hot = (spots[None, :] == spot.reshape(-1, 1)).astype(jnp.bfloat16)
                    out = out + jnp.dot(hot, back, preferred_element_type=jnp.float32)
                return out.astype(jnp.bfloat16)

            return branch

        return lax.switch(
            level,
            [at_level(*sizes) for sizes in levels],
            tokens,
            mate_tokens,
            info,
            goes_to,
            within,
            infos,
            first_arrived,
            kept_down,
            near_down,
            far_down,
            up,
            mate_up,
            base_value_matrix,
        )

    return local


def solution(mesh):
    in_specs = (
        P(("grp", "own"), None),
        P(("grp", "own"), None),
        P("grp"),
        P(),
        P(("grp", "own"), None, None),
        P(("grp", "own"), None, None),
    )
    out_specs = P(("grp", "own"), None)
    return jax.shard_map(
        make_local(dict(mesh.shape)),
        mesh=mesh,
        in_specs=in_specs,
        out_specs=out_specs,
        check_vma=False,
    )
```

```python
import functools

import jax
import jax.numpy as jnp
from jax import lax
from jax.experimental import pallas as pl
from jax.experimental.pallas import tpu as pltpu
from jax.sharding import PartitionSpec as P

LANES = 4
MATMUL_T = (((1,), (1,)), ((), ()))
PARAMS = pltpu.CompilerParams(vmem_limit_bytes=12 * 1024 * 1024)


def tile_of(width):
    return next(t for t in (2048, 1024, 512, 256, 128, width) if width % t == 0)


def level_body(starts, levels, first, place_ref, mine_ref, mate_ref, out_ref):
    mine, mate = mine_ref[...], mate_ref[...]
    planes = mine.shape[0]
    row = lax.broadcasted_iota(jnp.int32, (planes, 1), 0)
    source = jnp.bitwise_xor(row, place_ref[1])
    level = jnp.zeros((planes, 1), jnp.int32)
    for p, (low, high) in enumerate(starts):
        counts = []
        for packed in (mine, mate):
            here = jnp.where((packed >= low) & (packed < high), 1.0, 0.0)
            number = jnp.sum(here, axis=1, keepdims=True).astype(jnp.int32) - first
            counts.append(jnp.maximum(jnp.where(source == p, 0, number), 0))
        chip_rows, device_rows = counts[0] + counts[1], jnp.maximum(*counts)
        needed = jnp.zeros((planes, 1), jnp.int32)
        for chip_cap, device_cap in levels[:-1]:
            needed += jnp.where((chip_rows > chip_cap) | (device_rows > device_cap), 1, 0)
        level = jnp.maximum(level, needed)
    highest = level[0:1, :]
    for k in range(1, planes):
        highest = jnp.maximum(highest, level[k : k + 1, :])
    out_ref[...] = jnp.broadcast_to(highest, out_ref.shape)


def level_of(place, mine, mate, starts, levels, first):
    return pl.pallas_call(
        functools.partial(level_body, starts, levels, first),
        out_shape=jax.ShapeDtypeStruct((1, mine.shape[1]), jnp.int32),
        in_specs=[
            pl.BlockSpec(memory_space=pltpu.SMEM),
            pl.BlockSpec(memory_space=pltpu.VMEM),
            pl.BlockSpec(memory_space=pltpu.VMEM),
        ],
        out_specs=pl.BlockSpec(memory_space=pltpu.VMEM),
    )(place, mine, mate)


def pack_body(flips, number, start, place_ref, goes_ref, within_ref, *refs):
    core, plane, back = place_ref[0], place_ref[1], place_ref[2]
    values, outs, hot = refs[:number], refs[number:-1], refs[-1]
    size, rows = outs[0].shape[0], values[0].shape[0]

    @pl.when(pl.program_id(0) == 0)
    def _():
        spots = lax.broadcasted_iota(jnp.int32, (size, rows), 0)
        parts = []
        for flip in flips:
            to = jnp.bitwise_xor(plane, flip)
            sides = []
            for row in range(number):
                within = within_ref[row : row + 1, :] - start
                spot = within if number == 1 else jnp.where(core == row, within, back - 1 - within)
                named = (goes_ref[row : row + 1, :] == to) & (within >= 0) & (within < size)
                sides.append(jnp.where(spots == jnp.where(named, spot, -1), 1.0, 0.0))
            parts.append(jnp.concatenate(sides, axis=1))
        hot[...] = jnp.concatenate(parts, axis=0).astype(hot.dtype)

    rows_of_chip = jnp.concatenate([v[...] for v in values], axis=0)
    packed = jnp.dot(hot[...], rows_of_chip, preferred_element_type=jnp.float32)
    for i, out in enumerate(outs):
        out[...] = packed[i * size : (i + 1) * size, :].astype(out.dtype)


def pack(place, goes_to, within, values, start, size, flips):
    number, (rows, width) = len(values), values[0].shape
    width = width // number
    tile = tile_of(width)
    steps = width // tile
    whole = lambda a: pl.BlockSpec(a.shape, lambda k, place: (0, 0))
    strip = pl.BlockSpec(
        (rows, tile), lambda k, place: (0, k if number == 1 else place[0] * steps + k)
    )
    return pl.pallas_call(
        functools.partial(pack_body, flips, number, start),
        grid_spec=pltpu.PrefetchScalarGridSpec(
            num_scalar_prefetch=1,
            grid=(steps,),
            in_specs=[whole(goes_to), whole(within)] + [strip] * number,
            out_specs=[pl.BlockSpec((size, tile), lambda k, place: (0, k)) for _ in flips],
            scratch_shapes=[pltpu.VMEM((len(flips) * size, number * rows), values[0].dtype)],
        ),
        out_shape=[jax.ShapeDtypeStruct((size, width), values[0].dtype) for _ in flips],
        compiler_params=PARAMS,
        cost_estimate=pl.CostEstimate(
            flops=2 * len(flips) * size * number * rows * width,
            bytes_accessed=2 * width * (number * rows + len(flips) * size),
            transcendentals=0,
        ),
    )(place, goes_to, within, *values)


def shrink_body(number, maps, rank, start, place_ref, *refs):
    xs, ws = refs[:number], refs[number : number + maps]
    column, out, total = refs[number + maps :]
    step = pl.program_id(0)
    rows = jnp.concatenate([x[...] for x in xs], axis=0)
    weights = jnp.concatenate([w[...] for w in ws], axis=0)
    part = lax.dot_general(rows, weights, MATMUL_T, preferred_element_type=jnp.float32)

    @pl.when(step == 0)
    def _():
        total[...] = part

    @pl.when(step != 0)
    def _():
        total[...] += part

    @pl.when(step == pl.num_programs(0) - 1)
    def _():
        lanes = lax.broadcasted_iota(jnp.int32, total.shape, 1)
        low = (column[...] - start) * rank
        picked = jnp.where((lanes >= low) & (lanes < low + rank), total[...], 0.0)
        folded = picked[:, :rank]
        for q in range(1, total.shape[1] // rank):
            folded = folded + picked[:, q * rank : (q + 1) * rank]
        out[...] = folded


def shrink(place, xs, ws, column, rank, start=0):
    half = ws[0].shape[1]
    tile = tile_of(half)
    steps = half // tile
    rows, named = sum(x.shape[0] for x in xs), sum(w.shape[0] for w in ws)

    def strip(a):
        if a.shape[1] == half:
            return pl.BlockSpec((a.shape[0], tile), lambda k, place: (0, k))
        return pl.BlockSpec((a.shape[0], tile), lambda k, place: (0, place[0] * steps + k))

    return pl.pallas_call(
        functools.partial(shrink_body, len(xs), len(ws), rank, start),
        grid_spec=pltpu.PrefetchScalarGridSpec(
            num_scalar_prefetch=1,
            grid=(steps,),
            in_specs=[strip(x) for x in xs]
            + [strip(w) for w in ws]
            + [pl.BlockSpec(column.shape, lambda k, place: (0, 0))],
            out_specs=pl.BlockSpec((rows, rank), lambda k, place: (0, 0)),
            scratch_shapes=[pltpu.VMEM((rows, named), jnp.float32)],
        ),
        out_shape=jax.ShapeDtypeStruct((rows, rank), jnp.float32),
        compiler_params=PARAMS,
        cost_estimate=pl.CostEstimate(
            flops=2 * rows * named * half,
            bytes_accessed=2 * half * (rows + named),
            transcendentals=0,
        ),
    )(place, *xs, *ws, column)


def expand_body(chip_cap, device_cap, number, place_ref, one_ref, two_ref, column_ref, up_ref, *refs):
    given, outs = (refs[0], refs[1:]) if len(refs) > number else (None, refs)
    rank, named = one_ref.shape[1], up_ref.shape[0]
    row = lax.broadcasted_iota(jnp.int32, (rank, named), 0)
    lane = lax.broadcasted_iota(jnp.int32, (rank, named), 1)
    spread = jnp.zeros((rank, named), jnp.float32)
    for q in range(named // rank):
        spread = jnp.where(lane == row + q * rank, 1.0, spread)
    spread = spread.astype(jnp.bfloat16)

    def window(ref):
        parts = []
        for i in range(number):
            front, back = i * chip_cap, (i + 1) * chip_cap - device_cap
            a, b = ref[front : front + device_cap, :], ref[back : back + device_cap, :]
            parts.append(a if front == back else jnp.where(place_ref[0] == 0, a, b))
        return jnp.concatenate(parts, axis=0)

    shrunk = (window(one_ref) + window(two_ref)).astype(jnp.bfloat16)
    low = window(column_ref) * rank
    lanes = lax.broadcasted_iota(jnp.int32, (number * device_cap, named), 1)
    wide = jnp.dot(shrunk, spread, preferred_element_type=jnp.float32)
    wide = jnp.where((lanes >= low) & (lanes < low + rank), wide, 0.0).astype(jnp.bfloat16)
    delta = jnp.dot(wide, up_ref[...], preferred_element_type=jnp.float32)
    for i, out in enumerate(outs):
        mine = delta[i * device_cap : (i + 1) * device_cap, :].astype(out.dtype)
        if given is None:
            out[...] = mine
        else:
            first = out.shape[0] - device_cap
            out[...] = jnp.concatenate([given[i * first : (i + 1) * first, :], mine], axis=0)


def expand(place, one, two, column, up, number, device_cap, given=None):
    chip_cap = one.shape[0] // number
    rows = device_cap + (0 if given is None else given.shape[0] // number)
    operands = [place, one, two, column, up] + ([] if given is None else [given])
    return pl.pallas_call(
        functools.partial(expand_body, chip_cap, device_cap, number),
        in_specs=[pl.BlockSpec(memory_space=pltpu.SMEM)]
        + [pl.BlockSpec(memory_space=pltpu.VMEM) for _ in operands[1:]],
        out_specs=[pl.BlockSpec(memory_space=pltpu.VMEM) for _ in range(number)],
        out_shape=[jax.ShapeDtypeStruct((rows, up.shape[1]), up.dtype)] * number,
        compiler_params=PARAMS,
        cost_estimate=pl.CostEstimate(
            flops=2 * number * device_cap * up.shape[0] * up.shape[1],
            bytes_accessed=2 * up.size + 8 * one.size,
            transcendentals=0,
        ),
    )(*operands)


def make_local(mesh_shape):
    owners, groups = mesh_shape["own"], mesh_shape["grp"]
    planes = owners // LANES

    def flipped(x, axis, flip):
        size = mesh_shape[axis]
        return lax.ppermute(x, axis, [(i, i ^ flip) for i in range(size)])

    def swap(x, flip):
        return flipped(x, "own", flip)

    def send(x, flip):
        return flipped(x, "own", flip * LANES)

    def local(
        tokens,
        adapter_index_rows,
        adapter_pool_position,
        base_value_matrix,
        lowrank_down_weight,
        lowrank_up_weight,
    ):
        rows, width = tokens.shape
        held, rank, _ = lowrank_down_weight.shape
        out_width = base_value_matrix.shape[1]
        total = adapter_pool_position.shape[0]
        most = max(2, 2 * rows // total)
        cap = min(rows, LANES * held * most)
        first = cap // 4
        levels = [
            (2 * cap * chip // 16 - 2 * first, cap * device // 8 - first)
            for chip, device in ((10, 6), (11, 6), (12, 6), (13, 7), (16, 8))
        ]
        flips = sorted(range(1, planes), key=lambda k: -k)
        half = width // 2

        me = lax.axis_index("own")
        plane, lane, core = me // LANES, me % LANES, me % 2
        place = jnp.stack([core, plane, jnp.zeros_like(core)]).astype(jnp.int32)

        chosen = adapter_index_rows[:, 0]
        table = jnp.arange(total, dtype=jnp.int32)
        slot = jnp.sum(
            jnp.where(chosen[:, None] == table[None, :], adapter_pool_position[None, :], 0), axis=1
        )
        goes_to = slot // (held * LANES)
        places = jnp.arange(rows, dtype=jnp.int32)
        earlier = (goes_to[:, None] == goes_to[None, :]) & (places[None, :] < places[:, None])
        within = jnp.sum(earlier.astype(jnp.int32), axis=1)
        mine = (slot * rows + within)[None, :]

        down = lowrank_down_weight.reshape(held * rank, width)
        up = lowrank_up_weight.reshape(held * rank, out_width)
        half_of = lambda x, c: lax.dynamic_slice_in_dim(x, c * half, half, axis=1)
        mate_tokens, mate_down, mate_up = swap(tokens, 1), swap(down, 1), swap(up, 1)
        kept_down = half_of(down, core)
        far_down = swap(kept_down, 2)

        infos, step = mine, 1
        while step < planes:
            infos = jnp.concatenate([infos, send(infos, step)], axis=0)
            step *= 2
        first_rows = pack(place, goes_to[None, :], within[None, :], [tokens], 0, first, flips)
        infos, first_rows, mate_tokens, mate_down, mate_up = lax.optimization_barrier(
            (infos, first_rows, mate_tokens, mate_down, mate_up)
        )
        first_arrived = [send(x, k) for x, k in zip(first_rows, flips)]
        mate_infos = swap(infos, 1)
        span = rows * held * LANES
        starts = [(p * span, (p + 1) * span) for p in range(planes)]
        level = level_of(place, infos, mate_infos, starts, levels, first)
        level = jnp.maximum(level, swap(level, 2))
        step = 1
        while step < groups:
            level = jnp.maximum(level, flipped(level, "grp", step))
            step *= 2
        level = level[0, 0]
        infos = jnp.stack([infos, mate_infos], axis=1)
        info = infos[0]
        goes_to, within = info // span, info % rows
        near_down = lax.optimization_barrier(half_of(mate_down, core))

        def column_of(packed):
            slot = packed // rows
            return ((slot // held) % LANES ^ lane) * held + slot % held

        def at_level(chip_cap, device_cap):
            home_core = jnp.stack([core, 1 - core])[:, None]

            def spot_of(packed, size):
                ahead = packed % rows - first
                spot = jnp.where(home_core[: packed.shape[0]] == 0, ahead, size - 1 - ahead)
                return jnp.where(ahead >= 0, spot, -1)

            def named_by(spots, spot, column):
                hot = spots[:, None] == spot.reshape(1, -1)
                return jnp.sum(jnp.where(hot, column.reshape(1, -1) + 1, 0), 1, keepdims=True) - 1

            def branch(
                tokens,
                mate_tokens,
                info,
                goes_to,
                within,
                infos,
                first_arrived,
                kept_down,
                near_down,
                far_down,
                up,
                mate_up,
                matrix,
            ):
                packed = pack(
                    jnp.stack([core, plane, jnp.full_like(core, chip_cap)]),
                    goes_to,
                    within,
                    [tokens, mate_tokens],
                    first,
                    chip_cap,
                    flips,
                )
                packed, first_arrived, up, tokens, infos = lax.optimization_barrier(
                    (packed, first_arrived, up, tokens, infos)
                )
                arrived = [send(x, k) for x, k in zip(packed, flips)]
                last_down = swap(near_down, 2)
                down = [kept_down, near_down, far_down, last_down]
                up = jnp.concatenate([up, mate_up], axis=0)
                up = jnp.concatenate([up, swap(up, 2)], axis=0)
                first_mine = jnp.concatenate(first_arrived, axis=0)
                first_mate = swap(first_mine, 1)

                base = jnp.dot(tokens, matrix, preferred_element_type=jnp.float32)
                columns, first_columns = [], [[], []]
                for k in flips:
                    got = infos[k]
                    here = got // span == plane
                    columns.append(
                        named_by(
                            jnp.arange(chip_cap, dtype=jnp.int32),
                            jnp.where(here, spot_of(got, chip_cap), -1),
                            column_of(got),
                        )
                    )
                    for row in range(2):
                        first_columns[row].append(
                            named_by(
                                jnp.arange(first, dtype=jnp.int32),
                                jnp.where(here, got % rows, -1)[row],
                                column_of(got)[row],
                            )
                        )
                columns = jnp.concatenate(columns, axis=0)
                stays = jnp.where(goes_to == plane, column_of(info), -1)[:, :, None]
                own_columns = jnp.concatenate([stays[0]] + first_columns[0], axis=0)
                mate_columns = jnp.concatenate([stays[1]] + first_columns[1], axis=0)
                held_rows = own_columns.shape[0]
                rows_here = [tokens, first_mine, mate_tokens, first_mate]
                columns_here = jnp.concatenate([own_columns, mate_columns], axis=0)
                sums = shrink(place, rows_here, down[:3], columns_here, rank)
                sums = sums + shrink(place, rows_here, down[3:], columns_here, rank, 3 * held)
                (delta,) = expand(
                    place,
                    sums[:held_rows],
                    swap(sums[held_rows:], 1),
                    own_columns,
                    up,
                    1,
                    held_rows,
                )
                out = base + delta[:rows].astype(jnp.float32)
                arrived, columns, out, first_delta = lax.optimization_barrier(
                    (arrived, columns, out, delta[rows:])
                )

                sums = shrink(place, arrived, down, columns, rank)
                deltas = expand(
                    place,
                    sums,
                    swap(sums, 1),
                    columns,
                    up,
                    len(flips),
                    device_cap,
                    first_delta,
                )
                home = [send(x, k) for x, k in zip(deltas, flips)]
                spots = jnp.arange(first + device_cap, dtype=jnp.int32)
                for k, back in zip(flips, home):
                    ahead = info[:1] % rows
                    rest = spot_of(info[:1], device_cap) + first
                    spot = jnp.where(ahead < first, ahead, rest)
                    spot = jnp.where(goes_to[:1] == plane ^ k, spot, -1)
                    hot = (spots[None, :] == spot.reshape(-1, 1)).astype(jnp.bfloat16)
                    out = out + jnp.dot(hot, back, preferred_element_type=jnp.float32)
                return out.astype(jnp.bfloat16)

            return branch

        return lax.switch(
            level,
            [at_level(*sizes) for sizes in levels],
            tokens,
            mate_tokens,
            info,
            goes_to,
            within,
            infos,
            first_arrived,
            kept_down,
            near_down,
            far_down,
            up,
            mate_up,
            base_value_matrix,
        )

    return local


def solution(mesh):
    in_specs = (
        P(("grp", "own"), None),
        P(("grp", "own"), None),
        P("grp"),
        P(),
        P(("grp", "own"), None, None),
        P(("grp", "own"), None, None),
    )
    out_specs = P(("grp", "own"), None)
    return jax.shard_map(
        make_local(dict(mesh.shape)),
        mesh=mesh,
        in_specs=in_specs,
        out_specs=out_specs,
        check_vma=False,
    )
```

```python
import functools

import jax
import jax.numpy as jnp
from jax import lax
from jax.experimental import pallas as pl
from jax.experimental.pallas import tpu as pltpu
from jax.sharding import PartitionSpec as P

LANES = 4
MATMUL_T = (((1,), (1,)), ((), ()))
PARAMS = pltpu.CompilerParams(vmem_limit_bytes=12 * 1024 * 1024)


def tile_of(width):
    return next(t for t in (2048, 1024, 512, 256, 128, width) if width % t == 0)


def level_body(starts, levels, first, place_ref, mine_ref, mate_ref, out_ref):
    mine, mate = mine_ref[...], mate_ref[...]
    planes = mine.shape[0]
    row = lax.broadcasted_iota(jnp.int32, (planes, 1), 0)
    source = jnp.bitwise_xor(row, place_ref[1])
    level = jnp.zeros((planes, 1), jnp.int32)
    for p, (low, high) in enumerate(starts):
        counts = []
        for packed in (mine, mate):
            here = jnp.where((packed >= low) & (packed < high), 1.0, 0.0)
            number = jnp.sum(here, axis=1, keepdims=True).astype(jnp.int32) - first
            counts.append(jnp.maximum(jnp.where(source == p, 0, number), 0))
        chip_rows, device_rows = counts[0] + counts[1], jnp.maximum(*counts)
        needed = jnp.zeros((planes, 1), jnp.int32)
        for chip_cap, device_cap in levels[:-1]:
            needed += jnp.where((chip_rows > chip_cap) | (device_rows > device_cap), 1, 0)
        level = jnp.maximum(level, needed)
    highest = level[0:1, :]
    for k in range(1, planes):
        highest = jnp.maximum(highest, level[k : k + 1, :])
    out_ref[...] = jnp.broadcast_to(highest, out_ref.shape)


def level_of(place, mine, mate, starts, levels, first):
    return pl.pallas_call(
        functools.partial(level_body, starts, levels, first),
        out_shape=jax.ShapeDtypeStruct((1, mine.shape[1]), jnp.int32),
        in_specs=[
            pl.BlockSpec(memory_space=pltpu.SMEM),
            pl.BlockSpec(memory_space=pltpu.VMEM),
            pl.BlockSpec(memory_space=pltpu.VMEM),
        ],
        out_specs=pl.BlockSpec(memory_space=pltpu.VMEM),
    )(place, mine, mate)


def pack_body(flips, number, start, place_ref, goes_ref, within_ref, *refs):
    core, plane, back = place_ref[0], place_ref[1], place_ref[2]
    values, outs, hot = refs[:number], refs[number:-1], refs[-1]
    size, rows = outs[0].shape[0], values[0].shape[0]

    @pl.when(pl.program_id(0) == 0)
    def _():
        spots = lax.broadcasted_iota(jnp.int32, (size, rows), 0)
        parts = []
        for flip in flips:
            to = jnp.bitwise_xor(plane, flip)
            sides = []
            for row in range(number):
                within = within_ref[row : row + 1, :] - start
                spot = within if number == 1 else jnp.where(core == row, within, back - 1 - within)
                named = (goes_ref[row : row + 1, :] == to) & (within >= 0) & (within < size)
                sides.append(jnp.where(spots == jnp.where(named, spot, -1), 1.0, 0.0))
            parts.append(jnp.concatenate(sides, axis=1))
        hot[...] = jnp.concatenate(parts, axis=0).astype(hot.dtype)

    rows_of_chip = jnp.concatenate([v[...] for v in values], axis=0)
    packed = jnp.dot(hot[...], rows_of_chip, preferred_element_type=jnp.float32)
    for i, out in enumerate(outs):
        out[...] = packed[i * size : (i + 1) * size, :].astype(out.dtype)


def pack(place, goes_to, within, values, start, size, flips):
    number, (rows, width) = len(values), values[0].shape
    width = width // number
    tile = tile_of(width)
    steps = width // tile
    whole = lambda a: pl.BlockSpec(a.shape, lambda k, place: (0, 0))
    strip = pl.BlockSpec(
        (rows, tile), lambda k, place: (0, k if number == 1 else place[0] * steps + k)
    )
    return pl.pallas_call(
        functools.partial(pack_body, flips, number, start),
        grid_spec=pltpu.PrefetchScalarGridSpec(
            num_scalar_prefetch=1,
            grid=(steps,),
            in_specs=[whole(goes_to), whole(within)] + [strip] * number,
            out_specs=[pl.BlockSpec((size, tile), lambda k, place: (0, k)) for _ in flips],
            scratch_shapes=[pltpu.VMEM((len(flips) * size, number * rows), values[0].dtype)],
        ),
        out_shape=[jax.ShapeDtypeStruct((size, width), values[0].dtype) for _ in flips],
        compiler_params=PARAMS,
        cost_estimate=pl.CostEstimate(
            flops=2 * len(flips) * size * number * rows * width,
            bytes_accessed=2 * width * (number * rows + len(flips) * size),
            transcendentals=0,
        ),
    )(place, goes_to, within, *values)


def shrink_body(number, maps, rank, start, place_ref, *refs):
    xs, ws = refs[:number], refs[number : number + maps]
    column, out, total = refs[number + maps :]
    step = pl.program_id(0)
    rows = jnp.concatenate([x[...] for x in xs], axis=0)
    weights = jnp.concatenate([w[...] for w in ws], axis=0)
    part = lax.dot_general(rows, weights, MATMUL_T, preferred_element_type=jnp.float32)

    @pl.when(step == 0)
    def _():
        total[...] = part

    @pl.when(step != 0)
    def _():
        total[...] += part

    @pl.when(step == pl.num_programs(0) - 1)
    def _():
        lanes = lax.broadcasted_iota(jnp.int32, total.shape, 1)
        low = (column[...] - start) * rank
        picked = jnp.where((lanes >= low) & (lanes < low + rank), total[...], 0.0)
        folded = picked[:, :rank]
        for q in range(1, total.shape[1] // rank):
            folded = folded + picked[:, q * rank : (q + 1) * rank]
        out[...] = folded


def shrink(place, xs, ws, column, rank, start=0):
    half = ws[0].shape[1]
    tile = tile_of(half)
    steps = half // tile
    rows, named = sum(x.shape[0] for x in xs), sum(w.shape[0] for w in ws)

    def strip(a):
        if a.shape[1] == half:
            return pl.BlockSpec((a.shape[0], tile), lambda k, place: (0, k))
        return pl.BlockSpec((a.shape[0], tile), lambda k, place: (0, place[0] * steps + k))

    return pl.pallas_call(
        functools.partial(shrink_body, len(xs), len(ws), rank, start),
        grid_spec=pltpu.PrefetchScalarGridSpec(
            num_scalar_prefetch=1,
            grid=(steps,),
            in_specs=[strip(x) for x in xs]
            + [strip(w) for w in ws]
            + [pl.BlockSpec(column.shape, lambda k, place: (0, 0))],
            out_specs=pl.BlockSpec((rows, rank), lambda k, place: (0, 0)),
            scratch_shapes=[pltpu.VMEM((rows, named), jnp.float32)],
        ),
        out_shape=jax.ShapeDtypeStruct((rows, rank), jnp.float32),
        compiler_params=PARAMS,
        cost_estimate=pl.CostEstimate(
            flops=2 * rows * named * half,
            bytes_accessed=2 * half * (rows + named),
            transcendentals=0,
        ),
    )(place, *xs, *ws, column)


def expand_body(chip_cap, device_cap, number, place_ref, one_ref, two_ref, column_ref, up_ref, *refs):
    given, outs = (refs[0], refs[1:]) if len(refs) > number else (None, refs)
    rank, named = one_ref.shape[1], up_ref.shape[0]
    row = lax.broadcasted_iota(jnp.int32, (rank, named), 0)
    lane = lax.broadcasted_iota(jnp.int32, (rank, named), 1)
    spread = jnp.zeros((rank, named), jnp.float32)
    for q in range(named // rank):
        spread = jnp.where(lane == row + q * rank, 1.0, spread)
    spread = spread.astype(jnp.bfloat16)

    def window(ref):
        parts = []
        for i in range(number):
            front, back = i * chip_cap, (i + 1) * chip_cap - device_cap
            a, b = ref[front : front + device_cap, :], ref[back : back + device_cap, :]
            parts.append(a if front == back else jnp.where(place_ref[0] == 0, a, b))
        return jnp.concatenate(parts, axis=0)

    shrunk = (window(one_ref) + window(two_ref)).astype(jnp.bfloat16)
    low = window(column_ref) * rank
    lanes = lax.broadcasted_iota(jnp.int32, (number * device_cap, named), 1)
    wide = jnp.dot(shrunk, spread, preferred_element_type=jnp.float32)
    wide = jnp.where((lanes >= low) & (lanes < low + rank), wide, 0.0).astype(jnp.bfloat16)
    delta = jnp.dot(wide, up_ref[...], preferred_element_type=jnp.float32)
    for i, out in enumerate(outs):
        mine = delta[i * device_cap : (i + 1) * device_cap, :].astype(out.dtype)
        if given is None:
            out[...] = mine
        else:
            first = out.shape[0] - device_cap
            out[...] = jnp.concatenate([given[i * first : (i + 1) * first, :], mine], axis=0)


def expand(place, one, two, column, up, number, device_cap, given=None):
    chip_cap = one.shape[0] // number
    rows = device_cap + (0 if given is None else given.shape[0] // number)
    operands = [place, one, two, column, up] + ([] if given is None else [given])
    return pl.pallas_call(
        functools.partial(expand_body, chip_cap, device_cap, number),
        in_specs=[pl.BlockSpec(memory_space=pltpu.SMEM)]
        + [pl.BlockSpec(memory_space=pltpu.VMEM) for _ in operands[1:]],
        out_specs=[pl.BlockSpec(memory_space=pltpu.VMEM) for _ in range(number)],
        out_shape=[jax.ShapeDtypeStruct((rows, up.shape[1]), up.dtype)] * number,
        compiler_params=PARAMS,
        cost_estimate=pl.CostEstimate(
            flops=2 * number * device_cap * up.shape[0] * up.shape[1],
            bytes_accessed=2 * up.size + 8 * one.size,
            transcendentals=0,
        ),
    )(*operands)


def make_local(mesh_shape):
    owners, groups = mesh_shape["own"], mesh_shape["grp"]
    planes = owners // LANES

    def flipped(x, axis, flip):
        size = mesh_shape[axis]
        return lax.ppermute(x, axis, [(i, i ^ flip) for i in range(size)])

    def swap(x, flip):
        return flipped(x, "own", flip)

    def send(x, flip):
        return flipped(x, "own", flip * LANES)

    def local(
        tokens,
        adapter_index_rows,
        adapter_pool_position,
        base_value_matrix,
        lowrank_down_weight,
        lowrank_up_weight,
    ):
        rows, width = tokens.shape
        held, rank, _ = lowrank_down_weight.shape
        out_width = base_value_matrix.shape[1]
        total = adapter_pool_position.shape[0]
        most = max(2, 2 * rows // total)
        cap = min(rows, LANES * held * most)
        first = cap // 4
        levels = [
            (2 * cap * chip // 16 - 2 * first, cap * device // 8 - first)
            for chip, device in ((10, 6), (11, 6), (12, 6), (13, 7), (16, 8))
        ]
        flips = sorted(range(1, planes), key=lambda k: -k)
        half = width // 2

        me = lax.axis_index("own")
        plane, lane, core = me // LANES, me % LANES, me % 2
        place = jnp.stack([core, plane, jnp.zeros_like(core)]).astype(jnp.int32)

        chosen = adapter_index_rows[:, 0]
        table = jnp.arange(total, dtype=jnp.int32)
        slot = jnp.sum(
            jnp.where(chosen[:, None] == table[None, :], adapter_pool_position[None, :], 0), axis=1
        )
        goes_to = slot // (held * LANES)
        places = jnp.arange(rows, dtype=jnp.int32)
        earlier = (goes_to[:, None] == goes_to[None, :]) & (places[None, :] < places[:, None])
        within = jnp.sum(earlier.astype(jnp.int32), axis=1)
        mine = (slot * rows + within)[None, :]

        down = lowrank_down_weight.reshape(held * rank, width)
        up = lowrank_up_weight.reshape(held * rank, out_width)
        half_of = lambda x, c: lax.dynamic_slice_in_dim(x, c * half, half, axis=1)
        mate_tokens, mate_down, mate_up = swap(tokens, 1), swap(down, 1), swap(up, 1)
        kept_down = half_of(down, core)
        far_down = swap(kept_down, 2)

        infos, step = mine, 1
        while step < planes:
            infos = jnp.concatenate([infos, send(infos, step)], axis=0)
            step *= 2
        first_rows = pack(place, goes_to[None, :], within[None, :], [tokens], 0, first, flips)
        infos, first_rows, mate_tokens, mate_down, mate_up = lax.optimization_barrier(
            (infos, first_rows, mate_tokens, mate_down, mate_up)
        )
        first_arrived = [send(x, k) for x, k in zip(first_rows, flips)]
        mate_infos = swap(infos, 1)
        span = rows * held * LANES
        starts = [(p * span, (p + 1) * span) for p in range(planes)]
        level = level_of(place, infos, mate_infos, starts, levels, first)
        level = jnp.maximum(level, swap(level, 2))
        step = 1
        while step < groups:
            level = jnp.maximum(level, flipped(level, "grp", step))
            step *= 2
        level = level[0, 0]
        infos = jnp.stack([infos, mate_infos], axis=1)
        info = infos[0]
        goes_to, within = info // span, info % rows
        near_down = lax.optimization_barrier(half_of(mate_down, core))

        def column_of(packed):
            slot = packed // rows
            return ((slot // held) % LANES ^ lane) * held + slot % held

        def at_level(chip_cap, device_cap):
            home_core = jnp.stack([core, 1 - core])[:, None]

            def spot_of(packed, size):
                ahead = packed % rows - first
                spot = jnp.where(home_core[: packed.shape[0]] == 0, ahead, size - 1 - ahead)
                return jnp.where(ahead >= 0, spot, -1)

            def named_by(spots, spot, column):
                hot = spots[:, None] == spot.reshape(1, -1)
                return jnp.sum(jnp.where(hot, column.reshape(1, -1) + 1, 0), 1, keepdims=True) - 1

            def branch(
                tokens,
                mate_tokens,
                info,
                goes_to,
                within,
                infos,
                first_arrived,
                kept_down,
                near_down,
                far_down,
                up,
                mate_up,
                matrix,
            ):
                packed = pack(
                    jnp.stack([core, plane, jnp.full_like(core, chip_cap)]),
                    goes_to,
                    within,
                    [tokens, mate_tokens],
                    first,
                    chip_cap,
                    flips,
                )
                packed, first_arrived, up, tokens, infos = lax.optimization_barrier(
                    (packed, first_arrived, up, tokens, infos)
                )
                arrived = [send(x, k) for x, k in zip(packed, flips)]
                last_down = swap(near_down, 2)
                down = [kept_down, near_down, far_down, last_down]
                up = jnp.concatenate([up, mate_up], axis=0)
                up = jnp.concatenate([up, swap(up, 2)], axis=0)
                first_mine = jnp.concatenate(first_arrived, axis=0)
                first_mate = swap(first_mine, 1)

                columns, first_columns = [], [[], []]
                for k in flips:
                    got = infos[k]
                    here = got // span == plane
                    columns.append(
                        named_by(
                            jnp.arange(chip_cap, dtype=jnp.int32),
                            jnp.where(here, spot_of(got, chip_cap), -1),
                            column_of(got),
                        )
                    )
                    for row in range(2):
                        first_columns[row].append(
                            named_by(
                                jnp.arange(first, dtype=jnp.int32),
                                jnp.where(here, got % rows, -1)[row],
                                column_of(got)[row],
                            )
                        )
                columns = jnp.concatenate(columns, axis=0)
                stays = jnp.where(goes_to == plane, column_of(info), -1)[:, :, None]
                own_columns = jnp.concatenate([stays[0]] + first_columns[0], axis=0)
                mate_columns = jnp.concatenate([stays[1]] + first_columns[1], axis=0)
                held_rows = own_columns.shape[0]
                rows_here = [tokens, first_mine, mate_tokens, first_mate]
                columns_here = jnp.concatenate([own_columns, mate_columns], axis=0)
                sums = shrink(place, rows_here, down[:3], columns_here, rank)
                tokens, sums = lax.optimization_barrier((tokens, sums))
                base = jnp.dot(tokens, matrix, preferred_element_type=jnp.float32)
                base, last_down = lax.optimization_barrier((base, down[3]))
                sums = sums + shrink(place, rows_here, [last_down], columns_here, rank, 3 * held)
                (delta,) = expand(
                    place,
                    sums[:held_rows],
                    swap(sums[held_rows:], 1),
                    own_columns,
                    up,
                    1,
                    held_rows,
                )
                out = base + delta[:rows].astype(jnp.float32)
                arrived, columns, out, first_delta = lax.optimization_barrier(
                    (arrived, columns, out, delta[rows:])
                )

                sums = shrink(place, arrived, down, columns, rank)
                deltas = expand(
                    place,
                    sums,
                    swap(sums, 1),
                    columns,
                    up,
                    len(flips),
                    device_cap,
                    first_delta,
                )
                home = [send(x, k) for x, k in zip(deltas, flips)]
                spots = jnp.arange(first + device_cap, dtype=jnp.int32)
                for k, back in zip(flips, home):
                    ahead = info[:1] % rows
                    rest = spot_of(info[:1], device_cap) + first
                    spot = jnp.where(ahead < first, ahead, rest)
                    spot = jnp.where(goes_to[:1] == plane ^ k, spot, -1)
                    hot = (spots[None, :] == spot.reshape(-1, 1)).astype(jnp.bfloat16)
                    out = out + jnp.dot(hot, back, preferred_element_type=jnp.float32)
                return out.astype(jnp.bfloat16)

            return branch

        return lax.switch(
            level,
            [at_level(*sizes) for sizes in levels],
            tokens,
            mate_tokens,
            info,
            goes_to,
            within,
            infos,
            first_arrived,
            kept_down,
            near_down,
            far_down,
            up,
            mate_up,
            base_value_matrix,
        )

    return local


def solution(mesh):
    in_specs = (
        P(("grp", "own"), None),
        P(("grp", "own"), None),
        P("grp"),
        P(),
        P(("grp", "own"), None, None),
        P(("grp", "own"), None, None),
    )
    out_specs = P(("grp", "own"), None)
    return jax.shard_map(
        make_local(dict(mesh.shape)),
        mesh=mesh,
        in_specs=in_specs,
        out_specs=out_specs,
        check_vma=False,
    )
```

```python
import functools

import jax
import jax.numpy as jnp
from jax import lax
from jax.experimental import pallas as pl
from jax.experimental.pallas import tpu as pltpu
from jax.sharding import PartitionSpec as P

LANES = 4
MATMUL_T = (((1,), (1,)), ((), ()))
PARAMS = pltpu.CompilerParams(vmem_limit_bytes=12 * 1024 * 1024)


def tile_of(width):
    return next(t for t in (2048, 1024, 512, 256, 128, width) if width % t == 0)


def level_body(starts, levels, first, place_ref, mine_ref, mate_ref, out_ref):
    mine, mate = mine_ref[...], mate_ref[...]
    planes = mine.shape[0]
    row = lax.broadcasted_iota(jnp.int32, (planes, 1), 0)
    source = jnp.bitwise_xor(row, place_ref[1])
    level = jnp.zeros((planes, 1), jnp.int32)
    for p, (low, high) in enumerate(starts):
        counts = []
        for packed in (mine, mate):
            here = jnp.where((packed >= low) & (packed < high), 1.0, 0.0)
            number = jnp.sum(here, axis=1, keepdims=True).astype(jnp.int32) - first
            counts.append(jnp.maximum(jnp.where(source == p, 0, number), 0))
        chip_rows, device_rows = counts[0] + counts[1], jnp.maximum(*counts)
        needed = jnp.zeros((planes, 1), jnp.int32)
        for chip_cap, device_cap in levels[:-1]:
            needed += jnp.where((chip_rows > chip_cap) | (device_rows > device_cap), 1, 0)
        level = jnp.maximum(level, needed)
    highest = level[0:1, :]
    for k in range(1, planes):
        highest = jnp.maximum(highest, level[k : k + 1, :])
    out_ref[...] = jnp.broadcast_to(highest, out_ref.shape)


def level_of(place, mine, mate, starts, levels, first):
    return pl.pallas_call(
        functools.partial(level_body, starts, levels, first),
        out_shape=jax.ShapeDtypeStruct((1, mine.shape[1]), jnp.int32),
        in_specs=[
            pl.BlockSpec(memory_space=pltpu.SMEM),
            pl.BlockSpec(memory_space=pltpu.VMEM),
            pl.BlockSpec(memory_space=pltpu.VMEM),
        ],
        out_specs=pl.BlockSpec(memory_space=pltpu.VMEM),
    )(place, mine, mate)


def pack_body(flips, number, start, place_ref, goes_ref, within_ref, *refs):
    core, plane, back = place_ref[0], place_ref[1], place_ref[2]
    values, outs, hot = refs[:number], refs[number:-1], refs[-1]
    size, rows = outs[0].shape[0], values[0].shape[0]

    @pl.when(pl.program_id(0) == 0)
    def _():
        spots = lax.broadcasted_iota(jnp.int32, (size, rows), 0)
        parts = []
        for flip in flips:
            to = jnp.bitwise_xor(plane, flip)
            sides = []
            for row in range(number):
                within = within_ref[row : row + 1, :] - start
                spot = within if number == 1 else jnp.where(core == row, within, back - 1 - within)
                named = (goes_ref[row : row + 1, :] == to) & (within >= 0) & (within < size)
                sides.append(jnp.where(spots == jnp.where(named, spot, -1), 1.0, 0.0))
            parts.append(jnp.concatenate(sides, axis=1))
        hot[...] = jnp.concatenate(parts, axis=0).astype(hot.dtype)

    rows_of_chip = jnp.concatenate([v[...] for v in values], axis=0)
    packed = jnp.dot(hot[...], rows_of_chip, preferred_element_type=jnp.float32)
    for i, out in enumerate(outs):
        out[...] = packed[i * size : (i + 1) * size, :].astype(out.dtype)


def pack(place, goes_to, within, values, start, size, flips):
    number, (rows, width) = len(values), values[0].shape
    width = width // number
    tile = tile_of(width)
    steps = width // tile
    whole = lambda a: pl.BlockSpec(a.shape, lambda k, place: (0, 0))
    strip = pl.BlockSpec(
        (rows, tile), lambda k, place: (0, k if number == 1 else place[0] * steps + k)
    )
    return pl.pallas_call(
        functools.partial(pack_body, flips, number, start),
        grid_spec=pltpu.PrefetchScalarGridSpec(
            num_scalar_prefetch=1,
            grid=(steps,),
            in_specs=[whole(goes_to), whole(within)] + [strip] * number,
            out_specs=[pl.BlockSpec((size, tile), lambda k, place: (0, k)) for _ in flips],
            scratch_shapes=[pltpu.VMEM((len(flips) * size, number * rows), values[0].dtype)],
        ),
        out_shape=[jax.ShapeDtypeStruct((size, width), values[0].dtype) for _ in flips],
        compiler_params=PARAMS,
        cost_estimate=pl.CostEstimate(
            flops=2 * len(flips) * size * number * rows * width,
            bytes_accessed=2 * width * (number * rows + len(flips) * size),
            transcendentals=0,
        ),
    )(place, goes_to, within, *values)


def shrink_body(number, maps, rank, start, place_ref, *refs):
    xs, ws = refs[:number], refs[number : number + maps]
    column, out, total = refs[number + maps :]
    step = pl.program_id(0)
    rows = jnp.concatenate([x[...] for x in xs], axis=0)
    weights = jnp.concatenate([w[...] for w in ws], axis=0)
    part = lax.dot_general(rows, weights, MATMUL_T, preferred_element_type=jnp.float32)

    @pl.when(step == 0)
    def _():
        total[...] = part

    @pl.when(step != 0)
    def _():
        total[...] += part

    @pl.when(step == pl.num_programs(0) - 1)
    def _():
        lanes = lax.broadcasted_iota(jnp.int32, total.shape, 1)
        low = (column[...] - start) * rank
        picked = jnp.where((lanes >= low) & (lanes < low + rank), total[...], 0.0)
        folded = picked[:, :rank]
        for q in range(1, total.shape[1] // rank):
            folded = folded + picked[:, q * rank : (q + 1) * rank]
        out[...] = folded


def shrink(place, xs, ws, column, rank, start=0):
    half = ws[0].shape[1]
    tile = tile_of(half)
    steps = half // tile
    rows, named = sum(x.shape[0] for x in xs), sum(w.shape[0] for w in ws)

    def strip(a):
        if a.shape[1] == half:
            return pl.BlockSpec((a.shape[0], tile), lambda k, place: (0, k))
        return pl.BlockSpec((a.shape[0], tile), lambda k, place: (0, place[0] * steps + k))

    return pl.pallas_call(
        functools.partial(shrink_body, len(xs), len(ws), rank, start),
        grid_spec=pltpu.PrefetchScalarGridSpec(
            num_scalar_prefetch=1,
            grid=(steps,),
            in_specs=[strip(x) for x in xs]
            + [strip(w) for w in ws]
            + [pl.BlockSpec(column.shape, lambda k, place: (0, 0))],
            out_specs=pl.BlockSpec((rows, rank), lambda k, place: (0, 0)),
            scratch_shapes=[pltpu.VMEM((rows, named), jnp.float32)],
        ),
        out_shape=jax.ShapeDtypeStruct((rows, rank), jnp.float32),
        compiler_params=PARAMS,
        cost_estimate=pl.CostEstimate(
            flops=2 * rows * named * half,
            bytes_accessed=2 * half * (rows + named),
            transcendentals=0,
        ),
    )(place, *xs, *ws, column)


def expand_body(chip_cap, device_cap, number, place_ref, one_ref, two_ref, column_ref, up_ref, *refs):
    given, outs = (refs[0], refs[1:]) if len(refs) > number else (None, refs)
    rank, named = one_ref.shape[1], up_ref.shape[0]
    row = lax.broadcasted_iota(jnp.int32, (rank, named), 0)
    lane = lax.broadcasted_iota(jnp.int32, (rank, named), 1)
    spread = jnp.zeros((rank, named), jnp.float32)
    for q in range(named // rank):
        spread = jnp.where(lane == row + q * rank, 1.0, spread)
    spread = spread.astype(jnp.bfloat16)

    def window(ref):
        parts = []
        for i in range(number):
            front, back = i * chip_cap, (i + 1) * chip_cap - device_cap
            a, b = ref[front : front + device_cap, :], ref[back : back + device_cap, :]
            parts.append(a if front == back else jnp.where(place_ref[0] == 0, a, b))
        return jnp.concatenate(parts, axis=0)

    shrunk = (window(one_ref) + window(two_ref)).astype(jnp.bfloat16)
    low = window(column_ref) * rank
    lanes = lax.broadcasted_iota(jnp.int32, (number * device_cap, named), 1)
    wide = jnp.dot(shrunk, spread, preferred_element_type=jnp.float32)
    wide = jnp.where((lanes >= low) & (lanes < low + rank), wide, 0.0).astype(jnp.bfloat16)
    delta = jnp.dot(wide, up_ref[...], preferred_element_type=jnp.float32)
    for i, out in enumerate(outs):
        mine = delta[i * device_cap : (i + 1) * device_cap, :].astype(out.dtype)
        if given is None:
            out[...] = mine
        else:
            first = out.shape[0] - device_cap
            out[...] = jnp.concatenate([given[i * first : (i + 1) * first, :], mine], axis=0)


def expand(place, one, two, column, up, number, device_cap, given=None):
    chip_cap = one.shape[0] // number
    rows = device_cap + (0 if given is None else given.shape[0] // number)
    operands = [place, one, two, column, up] + ([] if given is None else [given])
    return pl.pallas_call(
        functools.partial(expand_body, chip_cap, device_cap, number),
        in_specs=[pl.BlockSpec(memory_space=pltpu.SMEM)]
        + [pl.BlockSpec(memory_space=pltpu.VMEM) for _ in operands[1:]],
        out_specs=[pl.BlockSpec(memory_space=pltpu.VMEM) for _ in range(number)],
        out_shape=[jax.ShapeDtypeStruct((rows, up.shape[1]), up.dtype)] * number,
        compiler_params=PARAMS,
        cost_estimate=pl.CostEstimate(
            flops=2 * number * device_cap * up.shape[0] * up.shape[1],
            bytes_accessed=2 * up.size + 8 * one.size,
            transcendentals=0,
        ),
    )(*operands)


def make_local(mesh_shape):
    owners, groups = mesh_shape["own"], mesh_shape["grp"]
    planes = owners // LANES

    def flipped(x, axis, flip):
        size = mesh_shape[axis]
        return lax.ppermute(x, axis, [(i, i ^ flip) for i in range(size)])

    def swap(x, flip):
        return flipped(x, "own", flip)

    def send(x, flip):
        return flipped(x, "own", flip * LANES)

    def local(
        tokens,
        adapter_index_rows,
        adapter_pool_position,
        base_value_matrix,
        lowrank_down_weight,
        lowrank_up_weight,
    ):
        rows, width = tokens.shape
        held, rank, _ = lowrank_down_weight.shape
        out_width = base_value_matrix.shape[1]
        total = adapter_pool_position.shape[0]
        most = max(2, 2 * rows // total)
        cap = min(rows, LANES * held * most)
        first = cap // 4
        levels = [
            (2 * cap * chip // 16 - 2 * first, cap * device // 8 - first)
            for chip, device in ((10, 6), (11, 6), (12, 6), (13, 7), (16, 8))
        ]
        flips = sorted(range(1, planes), key=lambda k: (k == 1, k))
        half = width // 2

        me = lax.axis_index("own")
        plane, lane, core = me // LANES, me % LANES, me % 2
        place = jnp.stack([core, plane, jnp.zeros_like(core)]).astype(jnp.int32)

        chosen = adapter_index_rows[:, 0]
        table = jnp.arange(total, dtype=jnp.int32)
        slot = jnp.sum(
            jnp.where(chosen[:, None] == table[None, :], adapter_pool_position[None, :], 0), axis=1
        )
        goes_to = slot // (held * LANES)
        places = jnp.arange(rows, dtype=jnp.int32)
        earlier = (goes_to[:, None] == goes_to[None, :]) & (places[None, :] < places[:, None])
        within = jnp.sum(earlier.astype(jnp.int32), axis=1)
        mine = (slot * rows + within)[None, :]

        down = lowrank_down_weight.reshape(held * rank, width)
        up = lowrank_up_weight.reshape(held * rank, out_width)
        half_of = lambda x, c: lax.dynamic_slice_in_dim(x, c * half, half, axis=1)
        mate_tokens, mate_down, mate_up = swap(tokens, 1), swap(down, 1), swap(up, 1)
        kept_down = half_of(down, core)
        far_down = swap(kept_down, 2)

        infos, step = mine, 1
        while step < planes:
            infos = jnp.concatenate([infos, send(infos, step)], axis=0)
            step *= 2
        first_rows = pack(place, goes_to[None, :], within[None, :], [tokens], 0, first, flips)
        infos, first_rows, mate_tokens, mate_down, mate_up = lax.optimization_barrier(
            (infos, first_rows, mate_tokens, mate_down, mate_up)
        )
        first_arrived = [send(x, k) for x, k in zip(first_rows, flips)]
        mate_infos = swap(infos, 1)
        span = rows * held * LANES
        starts = [(p * span, (p + 1) * span) for p in range(planes)]
        level = level_of(place, infos, mate_infos, starts, levels, first)
        level = jnp.maximum(level, swap(level, 2))
        step = 1
        while step < groups:
            level = jnp.maximum(level, flipped(level, "grp", step))
            step *= 2
        level = level[0, 0]
        infos = jnp.stack([infos, mate_infos], axis=1)
        info = infos[0]
        goes_to, within = info // span, info % rows
        near_down = lax.optimization_barrier(half_of(mate_down, core))

        def column_of(packed):
            slot = packed // rows
            return ((slot // held) % LANES ^ lane) * held + slot % held

        def at_level(chip_cap, device_cap):
            home_core = jnp.stack([core, 1 - core])[:, None]

            def spot_of(packed, size):
                ahead = packed % rows - first
                spot = jnp.where(home_core[: packed.shape[0]] == 0, ahead, size - 1 - ahead)
                return jnp.where(ahead >= 0, spot, -1)

            def named_by(spots, spot, column):
                hot = spots[:, None] == spot.reshape(1, -1)
                return jnp.sum(jnp.where(hot, column.reshape(1, -1) + 1, 0), 1, keepdims=True) - 1

            def branch(
                tokens,
                mate_tokens,
                info,
                goes_to,
                within,
                infos,
                first_arrived,
                kept_down,
                near_down,
                far_down,
                up,
                mate_up,
                matrix,
            ):
                packed = pack(
                    jnp.stack([core, plane, jnp.full_like(core, chip_cap)]),
                    goes_to,
                    within,
                    [tokens, mate_tokens],
                    first,
                    chip_cap,
                    flips,
                )
                packed, first_arrived, up, tokens, infos = lax.optimization_barrier(
                    (packed, first_arrived, up, tokens, infos)
                )
                arrived = [send(x, k) for x, k in zip(packed, flips)]
                last_down = swap(near_down, 2)
                down = [kept_down, near_down, far_down, last_down]
                up = jnp.concatenate([up, mate_up], axis=0)
                up = jnp.concatenate([up, swap(up, 2)], axis=0)
                first_mine = jnp.concatenate(first_arrived, axis=0)
                first_mate = swap(first_mine, 1)

                columns, first_columns = [], [[], []]
                for k in flips:
                    got = infos[k]
                    here = got // span == plane
                    columns.append(
                        named_by(
                            jnp.arange(chip_cap, dtype=jnp.int32),
                            jnp.where(here, spot_of(got, chip_cap), -1),
                            column_of(got),
                        )
                    )
                    for row in range(2):
                        first_columns[row].append(
                            named_by(
                                jnp.arange(first, dtype=jnp.int32),
                                jnp.where(here, got % rows, -1)[row],
                                column_of(got)[row],
                            )
                        )
                columns = jnp.concatenate(columns, axis=0)
                stays = jnp.where(goes_to == plane, column_of(info), -1)[:, :, None]
                own_columns = jnp.concatenate([stays[0]] + first_columns[0], axis=0)
                mate_columns = jnp.concatenate([stays[1]] + first_columns[1], axis=0)
                held_rows = own_columns.shape[0]
                rows_here = [tokens, first_mine, mate_tokens, first_mate]
                columns_here = jnp.concatenate([own_columns, mate_columns], axis=0)
                sums = shrink(place, rows_here, down[:3], columns_here, rank)
                tokens, sums = lax.optimization_barrier((tokens, sums))
                base = jnp.dot(tokens, matrix, preferred_element_type=jnp.float32)
                base, last_down = lax.optimization_barrier((base, down[3]))
                sums = sums + shrink(place, rows_here, [last_down], columns_here, rank, 3 * held)
                (delta,) = expand(
                    place,
                    sums[:held_rows],
                    swap(sums[held_rows:], 1),
                    own_columns,
                    up,
                    1,
                    held_rows,
                )
                out = base + delta[:rows].astype(jnp.float32)
                arrived, columns, out, first_delta = lax.optimization_barrier(
                    (arrived, columns, out, delta[rows:])
                )

                sums = shrink(place, arrived, down, columns, rank)
                deltas = expand(
                    place,
                    sums,
                    swap(sums, 1),
                    columns,
                    up,
                    len(flips),
                    device_cap,
                    first_delta,
                )
                home = [send(x, k) for x, k in zip(deltas, flips)]
                spots = jnp.arange(first + device_cap, dtype=jnp.int32)
                for k, back in zip(flips, home):
                    ahead = info[:1] % rows
                    rest = spot_of(info[:1], device_cap) + first
                    spot = jnp.where(ahead < first, ahead, rest)
                    spot = jnp.where(goes_to[:1] == plane ^ k, spot, -1)
                    hot = (spots[None, :] == spot.reshape(-1, 1)).astype(jnp.bfloat16)
                    out = out + jnp.dot(hot, back, preferred_element_type=jnp.float32)
                return out.astype(jnp.bfloat16)

            return branch

        return lax.switch(
            level,
            [at_level(*sizes) for sizes in levels],
            tokens,
            mate_tokens,
            info,
            goes_to,
            within,
            infos,
            first_arrived,
            kept_down,
            near_down,
            far_down,
            up,
            mate_up,
            base_value_matrix,
        )

    return local


def solution(mesh):
    in_specs = (
        P(("grp", "own"), None),
        P(("grp", "own"), None),
        P("grp"),
        P(),
        P(("grp", "own"), None, None),
        P(("grp", "own"), None, None),
    )
    out_specs = P(("grp", "own"), None)
    return jax.shard_map(
        make_local(dict(mesh.shape)),
        mesh=mesh,
        in_specs=in_specs,
        out_specs=out_specs,
        check_vma=False,
    )
```

```python
import functools

import jax
import jax.numpy as jnp
from jax import lax
from jax.experimental import pallas as pl
from jax.experimental.pallas import tpu as pltpu
from jax.sharding import PartitionSpec as P

LANES = 4
MATMUL_T = (((1,), (1,)), ((), ()))
PARAMS = pltpu.CompilerParams(vmem_limit_bytes=12 * 1024 * 1024)


def tile_of(width):
    return next(t for t in (2048, 1024, 512, 256, 128, width) if width % t == 0)


def level_body(starts, levels, first, place_ref, mine_ref, mate_ref, out_ref):
    mine, mate = mine_ref[...], mate_ref[...]
    planes = mine.shape[0]
    row = lax.broadcasted_iota(jnp.int32, (planes, 1), 0)
    source = jnp.bitwise_xor(row, place_ref[1])
    level = jnp.zeros((planes, 1), jnp.int32)
    for p, (low, high) in enumerate(starts):
        counts = []
        for packed in (mine, mate):
            here = jnp.where((packed >= low) & (packed < high), 1.0, 0.0)
            number = jnp.sum(here, axis=1, keepdims=True).astype(jnp.int32) - first
            counts.append(jnp.maximum(jnp.where(source == p, 0, number), 0))
        chip_rows, device_rows = counts[0] + counts[1], jnp.maximum(*counts)
        needed = jnp.zeros((planes, 1), jnp.int32)
        for chip_cap, device_cap in levels[:-1]:
            needed += jnp.where((chip_rows > chip_cap) | (device_rows > device_cap), 1, 0)
        level = jnp.maximum(level, needed)
    highest = level[0:1, :]
    for k in range(1, planes):
        highest = jnp.maximum(highest, level[k : k + 1, :])
    out_ref[...] = jnp.broadcast_to(highest, out_ref.shape)


def level_of(place, mine, mate, starts, levels, first):
    return pl.pallas_call(
        functools.partial(level_body, starts, levels, first),
        out_shape=jax.ShapeDtypeStruct((1, mine.shape[1]), jnp.int32),
        in_specs=[
            pl.BlockSpec(memory_space=pltpu.SMEM),
            pl.BlockSpec(memory_space=pltpu.VMEM),
            pl.BlockSpec(memory_space=pltpu.VMEM),
        ],
        out_specs=pl.BlockSpec(memory_space=pltpu.VMEM),
    )(place, mine, mate)


def pack_body(flips, number, start, place_ref, goes_ref, within_ref, *refs):
    core, plane, back = place_ref[0], place_ref[1], place_ref[2]
    values, outs, hot = refs[:number], refs[number:-1], refs[-1]
    size, rows = outs[0].shape[0], values[0].shape[0]

    @pl.when(pl.program_id(0) == 0)
    def _():
        spots = lax.broadcasted_iota(jnp.int32, (size, rows), 0)
        parts = []
        for flip in flips:
            to = jnp.bitwise_xor(plane, flip)
            sides = []
            for row in range(number):
                within = within_ref[row : row + 1, :] - start
                spot = within if number == 1 else jnp.where(core == row, within, back - 1 - within)
                named = (goes_ref[row : row + 1, :] == to) & (within >= 0) & (within < size)
                sides.append(jnp.where(spots == jnp.where(named, spot, -1), 1.0, 0.0))
            parts.append(jnp.concatenate(sides, axis=1))
        hot[...] = jnp.concatenate(parts, axis=0).astype(hot.dtype)

    rows_of_chip = jnp.concatenate([v[...] for v in values], axis=0)
    packed = jnp.dot(hot[...], rows_of_chip, preferred_element_type=jnp.float32)
    for i, out in enumerate(outs):
        out[...] = packed[i * size : (i + 1) * size, :].astype(out.dtype)


def pack(place, goes_to, within, values, start, size, flips):
    number, (rows, width) = len(values), values[0].shape
    width = width // number
    tile = tile_of(width)
    steps = width // tile
    whole = lambda a: pl.BlockSpec(a.shape, lambda k, place: (0, 0))
    strip = pl.BlockSpec(
        (rows, tile), lambda k, place: (0, k if number == 1 else place[0] * steps + k)
    )
    return pl.pallas_call(
        functools.partial(pack_body, flips, number, start),
        grid_spec=pltpu.PrefetchScalarGridSpec(
            num_scalar_prefetch=1,
            grid=(steps,),
            in_specs=[whole(goes_to), whole(within)] + [strip] * number,
            out_specs=[pl.BlockSpec((size, tile), lambda k, place: (0, k)) for _ in flips],
            scratch_shapes=[pltpu.VMEM((len(flips) * size, number * rows), values[0].dtype)],
        ),
        out_shape=[jax.ShapeDtypeStruct((size, width), values[0].dtype) for _ in flips],
        compiler_params=PARAMS,
        cost_estimate=pl.CostEstimate(
            flops=2 * len(flips) * size * number * rows * width,
            bytes_accessed=2 * width * (number * rows + len(flips) * size),
            transcendentals=0,
        ),
    )(place, goes_to, within, *values)


def shrink_body(number, maps, rank, start, place_ref, *refs):
    xs, ws = refs[:number], refs[number : number + maps]
    column, out, total = refs[number + maps :]
    step = pl.program_id(0)
    rows = jnp.concatenate([x[...] for x in xs], axis=0)
    weights = jnp.concatenate([w[...] for w in ws], axis=0)
    part = lax.dot_general(rows, weights, MATMUL_T, preferred_element_type=jnp.float32)

    @pl.when(step == 0)
    def _():
        total[...] = part

    @pl.when(step != 0)
    def _():
        total[...] += part

    @pl.when(step == pl.num_programs(0) - 1)
    def _():
        lanes = lax.broadcasted_iota(jnp.int32, total.shape, 1)
        low = (column[...] - start) * rank
        picked = jnp.where((lanes >= low) & (lanes < low + rank), total[...], 0.0)
        folded = picked[:, :rank]
        for q in range(1, total.shape[1] // rank):
            folded = folded + picked[:, q * rank : (q + 1) * rank]
        out[...] = folded


def shrink(place, xs, ws, column, rank, start=0):
    half = ws[0].shape[1]
    tile = tile_of(half)
    steps = half // tile
    rows, named = sum(x.shape[0] for x in xs), sum(w.shape[0] for w in ws)

    def strip(a):
        if a.shape[1] == half:
            return pl.BlockSpec((a.shape[0], tile), lambda k, place: (0, k))
        return pl.BlockSpec((a.shape[0], tile), lambda k, place: (0, place[0] * steps + k))

    return pl.pallas_call(
        functools.partial(shrink_body, len(xs), len(ws), rank, start),
        grid_spec=pltpu.PrefetchScalarGridSpec(
            num_scalar_prefetch=1,
            grid=(steps,),
            in_specs=[strip(x) for x in xs]
            + [strip(w) for w in ws]
            + [pl.BlockSpec(column.shape, lambda k, place: (0, 0))],
            out_specs=pl.BlockSpec((rows, rank), lambda k, place: (0, 0)),
            scratch_shapes=[pltpu.VMEM((rows, named), jnp.float32)],
        ),
        out_shape=jax.ShapeDtypeStruct((rows, rank), jnp.float32),
        compiler_params=PARAMS,
        cost_estimate=pl.CostEstimate(
            flops=2 * rows * named * half,
            bytes_accessed=2 * half * (rows + named),
            transcendentals=0,
        ),
    )(place, *xs, *ws, column)


def expand_body(chip_cap, device_cap, number, place_ref, one_ref, two_ref, column_ref, up_ref, *refs):
    given, outs = (refs[0], refs[1:]) if len(refs) > number else (None, refs)
    rank, named = one_ref.shape[1], up_ref.shape[0]
    row = lax.broadcasted_iota(jnp.int32, (rank, named), 0)
    lane = lax.broadcasted_iota(jnp.int32, (rank, named), 1)
    spread = jnp.zeros((rank, named), jnp.float32)
    for q in range(named // rank):
        spread = jnp.where(lane == row + q * rank, 1.0, spread)
    spread = spread.astype(jnp.bfloat16)

    def window(ref):
        parts = []
        for i in range(number):
            front, back = i * chip_cap, (i + 1) * chip_cap - device_cap
            a, b = ref[front : front + device_cap, :], ref[back : back + device_cap, :]
            parts.append(a if front == back else jnp.where(place_ref[0] == 0, a, b))
        return jnp.concatenate(parts, axis=0)

    shrunk = (window(one_ref) + window(two_ref)).astype(jnp.bfloat16)
    low = window(column_ref) * rank
    lanes = lax.broadcasted_iota(jnp.int32, (number * device_cap, named), 1)
    wide = jnp.dot(shrunk, spread, preferred_element_type=jnp.float32)
    wide = jnp.where((lanes >= low) & (lanes < low + rank), wide, 0.0).astype(jnp.bfloat16)
    delta = jnp.dot(wide, up_ref[...], preferred_element_type=jnp.float32)
    for i, out in enumerate(outs):
        mine = delta[i * device_cap : (i + 1) * device_cap, :].astype(out.dtype)
        if given is None:
            out[...] = mine
        else:
            first = out.shape[0] - device_cap
            out[...] = jnp.concatenate([given[i * first : (i + 1) * first, :], mine], axis=0)


def expand(place, one, two, column, up, number, device_cap, given=None):
    chip_cap = one.shape[0] // number
    rows = device_cap + (0 if given is None else given.shape[0] // number)
    operands = [place, one, two, column, up] + ([] if given is None else [given])
    return pl.pallas_call(
        functools.partial(expand_body, chip_cap, device_cap, number),
        in_specs=[pl.BlockSpec(memory_space=pltpu.SMEM)]
        + [pl.BlockSpec(memory_space=pltpu.VMEM) for _ in operands[1:]],
        out_specs=[pl.BlockSpec(memory_space=pltpu.VMEM) for _ in range(number)],
        out_shape=[jax.ShapeDtypeStruct((rows, up.shape[1]), up.dtype)] * number,
        compiler_params=PARAMS,
        cost_estimate=pl.CostEstimate(
            flops=2 * number * device_cap * up.shape[0] * up.shape[1],
            bytes_accessed=2 * up.size + 8 * one.size,
            transcendentals=0,
        ),
    )(*operands)


def make_local(mesh_shape):
    owners, groups = mesh_shape["own"], mesh_shape["grp"]
    planes = owners // LANES

    def flipped(x, axis, flip):
        size = mesh_shape[axis]
        return lax.ppermute(x, axis, [(i, i ^ flip) for i in range(size)])

    def swap(x, flip):
        return flipped(x, "own", flip)

    def send(x, flip):
        return flipped(x, "own", flip * LANES)

    def local(
        tokens,
        adapter_index_rows,
        adapter_pool_position,
        base_value_matrix,
        lowrank_down_weight,
        lowrank_up_weight,
    ):
        rows, width = tokens.shape
        held, rank, _ = lowrank_down_weight.shape
        out_width = base_value_matrix.shape[1]
        total = adapter_pool_position.shape[0]
        most = max(2, 2 * rows // total)
        cap = min(rows, LANES * held * most)
        first = cap // 4
        levels = [
            (2 * cap * chip // 16 - 2 * first, cap * device // 8 - first)
            for chip, device in ((10, 6), (11, 6), (12, 6), (13, 7), (16, 8))
        ]
        flips = sorted(range(1, planes), key=lambda k: -k)
        half = width // 2

        me = lax.axis_index("own")
        plane, lane, core = me // LANES, me % LANES, me % 2
        place = jnp.stack([core, plane, jnp.zeros_like(core)]).astype(jnp.int32)

        chosen = adapter_index_rows[:, 0]
        table = jnp.arange(total, dtype=jnp.int32)
        slot = jnp.sum(
            jnp.where(chosen[:, None] == table[None, :], adapter_pool_position[None, :], 0), axis=1
        )
        goes_to = slot // (held * LANES)
        places = jnp.arange(rows, dtype=jnp.int32)
        earlier = (goes_to[:, None] == goes_to[None, :]) & (places[None, :] < places[:, None])
        within = jnp.sum(earlier.astype(jnp.int32), axis=1)
        mine = (slot * rows + within)[None, :]

        down = lowrank_down_weight.reshape(held * rank, width)
        up = lowrank_up_weight.reshape(held * rank, out_width)
        half_of = lambda x, c: lax.dynamic_slice_in_dim(x, c * half, half, axis=1)
        mate_tokens, mate_down, mate_up = swap(tokens, 1), swap(down, 1), swap(up, 1)
        kept_down = half_of(down, core)
        far_down = swap(kept_down, 2)

        infos, step = mine, 1
        while step < planes:
            infos = jnp.concatenate([infos, send(infos, step)], axis=0)
            step *= 2
        first_rows = pack(place, goes_to[None, :], within[None, :], [tokens], 0, first, flips)
        infos, first_rows, mate_tokens, mate_down, mate_up = lax.optimization_barrier(
            (infos, first_rows, mate_tokens, mate_down, mate_up)
        )
        first_arrived = [send(x, k) for x, k in zip(first_rows, flips)]
        mate_infos = swap(infos, 1)
        span = rows * held * LANES
        starts = [(p * span, (p + 1) * span) for p in range(planes)]
        level = level_of(place, infos, mate_infos, starts, levels, first)
        level = jnp.maximum(level, swap(level, 2))
        step = 1
        while step < groups:
            level = jnp.maximum(level, flipped(level, "grp", step))
            step *= 2
        level = level[0, 0]
        infos = jnp.stack([infos, mate_infos], axis=1)
        info = infos[0]
        goes_to, within = info // span, info % rows
        near_down = lax.optimization_barrier(half_of(mate_down, core))

        def column_of(packed):
            slot = packed // rows
            return ((slot // held) % LANES ^ lane) * held + slot % held

        def at_level(chip_cap, device_cap):
            home_core = jnp.stack([core, 1 - core])[:, None]

            def spot_of(packed, size):
                ahead = packed % rows - first
                spot = jnp.where(home_core[: packed.shape[0]] == 0, ahead, size - 1 - ahead)
                return jnp.where(ahead >= 0, spot, -1)

            def named_by(spots, spot, column):
                hot = spots[:, None] == spot.reshape(1, -1)
                return jnp.sum(jnp.where(hot, column.reshape(1, -1) + 1, 0), 1, keepdims=True) - 1

            def branch(
                tokens,
                mate_tokens,
                info,
                goes_to,
                within,
                infos,
                first_arrived,
                kept_down,
                near_down,
                far_down,
                up,
                mate_up,
                matrix,
            ):
                packed = pack(
                    jnp.stack([core, plane, jnp.full_like(core, chip_cap)]),
                    goes_to,
                    within,
                    [tokens, mate_tokens],
                    first,
                    chip_cap,
                    flips,
                )
                packed, first_arrived, up, tokens, infos = lax.optimization_barrier(
                    (packed, first_arrived, up, tokens, infos)
                )
                arrived = [send(x, k) for x, k in zip(packed, flips)]
                last_down = swap(near_down, 2)
                down = [kept_down, near_down, far_down, last_down]
                far_up = swap(up, 2)
                up = jnp.concatenate([up, mate_up, far_up, swap(far_up, 1)], axis=0)
                first_mine = jnp.concatenate(first_arrived, axis=0)
                first_mate = swap(first_mine, 1)

                columns, first_columns = [], [[], []]
                for k in flips:
                    got = infos[k]
                    here = got // span == plane
                    columns.append(
                        named_by(
                            jnp.arange(chip_cap, dtype=jnp.int32),
                            jnp.where(here, spot_of(got, chip_cap), -1),
                            column_of(got),
                        )
                    )
                    for row in range(2):
                        first_columns[row].append(
                            named_by(
                                jnp.arange(first, dtype=jnp.int32),
                                jnp.where(here, got % rows, -1)[row],
                                column_of(got)[row],
                            )
                        )
                columns = jnp.concatenate(columns, axis=0)
                stays = jnp.where(goes_to == plane, column_of(info), -1)[:, :, None]
                own_columns = jnp.concatenate([stays[0]] + first_columns[0], axis=0)
                mate_columns = jnp.concatenate([stays[1]] + first_columns[1], axis=0)
                held_rows = own_columns.shape[0]
                rows_here = [tokens, first_mine, mate_tokens, first_mate]
                columns_here = jnp.concatenate([own_columns, mate_columns], axis=0)
                sums = shrink(place, rows_here, down[:3], columns_here, rank)
                tokens, sums = lax.optimization_barrier((tokens, sums))
                base = jnp.dot(tokens, matrix, preferred_element_type=jnp.float32)
                base, last_down = lax.optimization_barrier((base, down[3]))
                sums = sums + shrink(place, rows_here, [last_down], columns_here, rank, 3 * held)
                (delta,) = expand(
                    place,
                    sums[:held_rows],
                    swap(sums[held_rows:], 1),
                    own_columns,
                    up,
                    1,
                    held_rows,
                )
                out = base + delta[:rows].astype(jnp.float32)
                arrived, columns, out, first_delta = lax.optimization_barrier(
                    (arrived, columns, out, delta[rows:])
                )

                sums = shrink(place, arrived, down, columns, rank)
                deltas = expand(
                    place,
                    sums,
                    swap(sums, 1),
                    columns,
                    up,
                    len(flips),
                    device_cap,
                    first_delta,
                )
                home = [send(x, k) for x, k in zip(deltas, flips)]
                spots = jnp.arange(first + device_cap, dtype=jnp.int32)
                for k, back in zip(flips, home):
                    ahead = info[:1] % rows
                    rest = spot_of(info[:1], device_cap) + first
                    spot = jnp.where(ahead < first, ahead, rest)
                    spot = jnp.where(goes_to[:1] == plane ^ k, spot, -1)
                    hot = (spots[None, :] == spot.reshape(-1, 1)).astype(jnp.bfloat16)
                    out = out + jnp.dot(hot, back, preferred_element_type=jnp.float32)
                return out.astype(jnp.bfloat16)

            return branch

        return lax.switch(
            level,
            [at_level(*sizes) for sizes in levels],
            tokens,
            mate_tokens,
            info,
            goes_to,
            within,
            infos,
            first_arrived,
            kept_down,
            near_down,
            far_down,
            up,
            mate_up,
            base_value_matrix,
        )

    return local


def solution(mesh):
    in_specs = (
        P(("grp", "own"), None),
        P(("grp", "own"), None),
        P("grp"),
        P(),
        P(("grp", "own"), None, None),
        P(("grp", "own"), None, None),
    )
    out_specs = P(("grp", "own"), None)
    return jax.shard_map(
        make_local(dict(mesh.shape)),
        mesh=mesh,
        in_specs=in_specs,
        out_specs=out_specs,
        check_vma=False,
    )
```
